32 devices in a mesh: dp: 4 (over y, x), expert: 8 (over z, core).
Axes of the slice: x: 2, y: 2, z: 4, core: 2. Of those that a mesh axis runs over, the one named last changes fastest.
Arguments:
- tokens: bfloat16 [4096, 4096], P(('dp', 'expert')), may hold values from -6 to 6
- out_grad: bfloat16 [4096, 4096], P(('dp', 'expert')), may hold values from -6 to 6
- route_slots: int32 [4, 8, 8, 64], P('dp', 'expert'), may hold values from -1 to 127, as said below
- expert_counts: int32 [4096], P(('dp', 'expert')), may hold values from 0 to 8, as said below
- router_weight: float32 [4096, 8], replicated, may hold values from -0.09375 to 0.09375
- up_weight: bfloat16 [8, 4096, 1024], P('expert'), may hold values from -0.09375 to 0.09375
- down_weight: bfloat16 [8, 4096, 1024], P('expert'), may hold values from -0.1875 to 0.1875
Outputs:
- tokens_grad: bfloat16 [4096, 4096], P(('dp', 'expert'))
- up_grad: bfloat16 [8, 4096, 1024], P('expert', 'dp')
- down_grad: bfloat16 [8, 4096, 1024], P('expert', 'dp')
- router_grad: float32 [4096, 8], P(None, 'expert')
The draws below stay inside these ranges and needn't reach their ends.
Inputs may be any that keep to these rules, and one draw needn't show every extreme that they name: In route_slots[p, s, e, :] the chosen local tokens are distinct and come first, then -1; every list holds at least one token. In every batch shard some expert takes 64 tokens from every device of it. On every device one local token is chosen by every expert. expert_counts of a token equals the number of lists of route_slots that hold it.
All inputs are finite; a program needn't handle non-finite values.
Results may differ from the reference program's by a relative error of at most 0.017.
Values may be sent and summed in bfloat16 or wider, within the bound.
No kernel may reach another device: no remote copies, remote signals or barrier semaphores. Data moves between devices by JAX's collectives and lax.ppermute only.
A program may use at most 192 MiB of HBM per device.

```python
import jax
import jax.numpy as jnp
from jax import lax

D = 4096
H = 1024
TOK_DEV = 128
EXPERTS = 8
RECV = 512
SLOT = 64
TOKENS = 4096
N_DP = 4
N_EXPERT = 8


def route_common(key):
    base = jax.random.fold_in(key, 7)
    key_count, key_full, key_perm, key_shared = jax.random.split(base, 4)
    counts = jax.random.randint(key_count, (N_DP, N_EXPERT, EXPERTS), 1, SLOT + 1)
    full = jax.random.randint(key_full, (N_DP,), 0, EXPERTS)
    chosen = jnp.arange(EXPERTS, dtype=jnp.int32)[None, None, :] == full[:, None, None]
    counts = jnp.where(chosen, SLOT, counts)
    shared = jax.random.randint(key_shared, (N_DP, N_EXPERT), 0, TOK_DEV).astype(jnp.int32)
    keys = jax.random.split(key_perm, N_DP * N_EXPERT * EXPERTS)
    perms = jax.vmap(lambda single: jax.random.permutation(single, TOK_DEV))(keys)
    perms = perms.reshape(N_DP, N_EXPERT, EXPERTS, TOK_DEV).astype(jnp.int32)
    hot = shared[:, :, None, None]
    first = perms[..., :1]
    perms = jnp.where(perms == hot, first, perms)
    places_all = jnp.arange(TOK_DEV, dtype=jnp.int32)[None, None, None, :]
    perms = jnp.where(places_all == 0, hot, perms)
    perms = perms[..., :SLOT]
    places = jnp.arange(SLOT, dtype=jnp.int32)[None, None, None, :]
    return jnp.where(places < counts[..., None], perms, -1).astype(jnp.int32)


def draw_route_slots(key, part):
    return route_common(key)


def draw_expert_counts(key, part):
    slots = route_common(key)
    hits = (slots[..., None] == jnp.arange(TOK_DEV, dtype=jnp.int32)).astype(jnp.int32)
    return jnp.sum(hits, axis=(2, 3)).reshape(TOKENS).astype(jnp.int32)


def steps_of(rng, dims, pieces, low, top_value):
    level, own = 1.0, jax.random.fold_in(rng, 6)
    for position, parts in pieces:
        heights = jnp.exp(jax.random.uniform(jax.random.fold_in(own, position), (parts,), jnp.float32, low / len(pieces), top_value / len(pieces)))
        level = level * jnp.repeat(heights, dims[position] // parts).reshape([-1 if axis == position else 1 for axis in range(len(dims))])
    return level


def gaussian(rng, dims, scale, most, cuts=(), held_as=jnp.bfloat16):
    values = jax.random.normal(rng, dims, jnp.float32) * scale
    if len(cuts) > 0:
        values = steps_of(rng, dims, cuts, -0.22, 0.18) * values
    return jnp.clip(values, min=-most, max=most).astype(held_as)


def setup_inputs(seed: int = 0) -> dict:
    key_of = jax.random.split(jax.random.key(seed), 8)
    return {
        "tokens": gaussian(key_of[0], (TOKENS, D), 1.0, 6.0, ((0, 32),)),
        "out_grad": gaussian(key_of[1], (TOKENS, D), 1.0, 6.0, ((0, 32),)),
        "route_slots": draw_route_slots(jax.random.fold_in(key_of[7], 71), 0),
        "expert_counts": draw_expert_counts(jax.random.fold_in(key_of[7], 71), 0),
        "router_weight": gaussian(key_of[4], (D, EXPERTS), D ** -0.5, 0.09375, (), jnp.float32),
        "up_weight": gaussian(key_of[5], (EXPERTS, D, H), D ** -0.5, 0.09375, ((0, 8),)),
        "down_weight": gaussian(key_of[6], (EXPERTS, D, H), H ** -0.5, 0.1875, ((0, 8),)),
    }


def gelu_pair(values):
    inner = 0.7978845608 * (values + 0.044715 * values * values * values)
    tangent = jnp.tanh(inner)
    result = 0.5 * values * (1.0 + tangent)
    slope = 0.5 * (1.0 + tangent) + 0.5 * values * (1.0 - tangent * tangent) * 0.7978845608 * (1.0 + 3.0 * 0.044715 * values * values)
    return result, slope


def reference(tokens, out_grad, route_slots, expert_counts, router_weight, up_weight, down_weight):
    group_rows = N_EXPERT * TOK_DEV
    width = tokens.shape[1]
    tok_groups = tokens.reshape(N_DP, group_rows, width)
    grad_groups = out_grad.reshape(N_DP, group_rows, width)
    count_groups = expert_counts.reshape(N_DP, group_rows).astype(jnp.float32)
    logits = jnp.dot(tokens.astype(jnp.float32), router_weight, precision=lax.Precision.HIGHEST)
    gates = jax.nn.sigmoid(logits).reshape(N_DP, group_rows, EXPERTS)
    source = (jnp.arange(N_EXPERT, dtype=jnp.int32) * TOK_DEV)[:, None]
    contract = (((0,), (0,)), ((), ()))
    trailing = (((1,), (1,)), ((), ()))

    def per_expert(carry, expert):
        row_acc, logit_acc = carry
        w_up = up_weight[expert]
        w_down = down_weight[expert]
        up_total = jnp.zeros((width, H), jnp.float32)
        down_total = jnp.zeros((width, H), jnp.float32)
        column = jnp.zeros((width,), jnp.float32)
        for group in range(N_DP):
            slots = route_slots[group, :, expert, :]
            valid = (slots >= 0).reshape(RECV)
            index = (source + jnp.maximum(slots, 0)).reshape(RECV).astype(jnp.int32)
            rows_in = jnp.where(valid[:, None], tok_groups[group][index], jnp.zeros((), tokens.dtype))
            grads_in = jnp.where(valid[:, None], grad_groups[group][index], jnp.zeros((), out_grad.dtype))
            gate_slot = jnp.where(valid, gates[group][index, expert], 0.0)
            count_slot = jnp.where(valid, count_groups[group][index], 1.0)
            weight_slot = jnp.where(valid, gate_slot / count_slot, 0.0)
            slope_slot = jnp.where(valid, gate_slot * (1.0 - gate_slot) / count_slot, 0.0)
            pre = jnp.dot(rows_in, w_up, preferred_element_type=jnp.float32)
            active, slope = gelu_pair(pre)
            active = active.astype(jnp.bfloat16)
            output = lax.dot_general(active, w_down, trailing, preferred_element_type=jnp.float32)
            score = jnp.sum(grads_in.astype(jnp.float32) * output, axis=1)
            out_scaled = (weight_slot[:, None] * grads_in.astype(jnp.float32)).astype(jnp.bfloat16)
            act_grad = jnp.dot(out_scaled, w_down, preferred_element_type=jnp.float32)
            pre_grad = (act_grad * slope).astype(jnp.bfloat16)
            row_grad = lax.dot_general(pre_grad, w_up, trailing, preferred_element_type=jnp.float32).astype(jnp.bfloat16)
            row_acc = row_acc.at[group, index].add(jnp.where(valid[:, None], row_grad.astype(jnp.float32), 0.0))
            logit_acc = logit_acc.at[group, index, expert].add(jnp.where(valid, score * slope_slot, 0.0))
            up_total = up_total + lax.dot_general(rows_in, pre_grad, contract, preferred_element_type=jnp.float32)
            down_total = down_total + lax.dot_general(out_scaled, active, contract, preferred_element_type=jnp.float32)
            column = column + jnp.dot(score * slope_slot, rows_in.astype(jnp.float32), precision=lax.Precision.HIGHEST)
        return (row_acc, logit_acc), (up_total.astype(jnp.bfloat16), down_total.astype(jnp.bfloat16), column)

    start = (jnp.zeros((N_DP, group_rows, width), jnp.float32), jnp.zeros((N_DP, group_rows, EXPERTS), jnp.float32))
    (row_acc, logit_acc), (up_grads, down_grads, columns) = lax.scan(per_expert, start, jnp.arange(EXPERTS, dtype=jnp.int32))
    logit_grad = logit_acc.reshape(TOKENS, EXPERTS)
    tokens_grad = (row_acc.reshape(TOKENS, width) + jnp.dot(logit_grad, router_weight.T, precision=lax.Precision.HIGHEST)).astype(jnp.bfloat16)
    return tokens_grad, up_grads, down_grads, columns.T
```

```python
import functools

import jax
import jax.numpy as jnp
from jax import lax
from jax.experimental import pallas as pl
from jax.experimental.pallas import tpu as pltpu
from jax.sharding import PartitionSpec as P

VMEM_LIMIT = 48 * 1024 * 1024


def gelu_pair(values):
    inner = 0.7978845608 * (values + 0.044715 * values * values * values)
    tangent = jnp.tanh(inner)
    result = 0.5 * values * (1.0 + tangent)
    slope = 0.5 * (1.0 + tangent) + 0.5 * values * (1.0 - tangent * tangent) * 0.7978845608 * (
        1.0 + 3.0 * 0.044715 * values * values
    )
    return (result, slope)


def gate_logits(tokens, router_weight):
    high = lax.reduce_precision(router_weight, 8, 7)
    rest = router_weight - high
    middle = lax.reduce_precision(rest, 8, 7)
    low = rest - middle
    terms = jnp.concatenate([high, middle, low], axis=1).astype(jnp.bfloat16)
    parts = jnp.dot(tokens, terms, preferred_element_type=jnp.float32)
    experts = router_weight.shape[1]
    return parts[:, :experts] + parts[:, experts : 2 * experts] + parts[:, 2 * experts :]


def hidden_kernel(
    meta_ref, t0_ref, t1_ref, g0_ref, g1_ref, up_ref, down_ref, xg_ref, dw_ref, lg_ref, pre, back
):
    step = pl.program_id(0)
    steps = pl.num_programs(0)
    rows = meta_ref.shape[0]
    half = rows // 2
    tok_rows = t0_ref.shape[0]
    places = lax.broadcasted_iota(jnp.int32, (rows, tok_rows), 1).astype(jnp.float32)
    picks = (meta_ref[:, 0:1] == places).astype(jnp.bfloat16)

    def pick(first, second):
        top = jnp.dot(picks[:half], first[...], preferred_element_type=jnp.float32)
        bottom = jnp.dot(picks[half:], second[...], preferred_element_type=jnp.float32)
        return jnp.concatenate([top, bottom], axis=0).astype(jnp.bfloat16)

    x = pick(t0_ref, t1_ref)
    g = pick(g0_ref, g1_ref)
    xg_ref[0, :rows] = x
    xg_ref[0, rows:] = g
    pre_term = jnp.dot(x, up_ref[...], preferred_element_type=jnp.float32)
    back_term = jnp.dot(g, down_ref[...], preferred_element_type=jnp.float32)

    @pl.when(step == 0)
    def _():
        pre[...] = pre_term
        back[...] = back_term

    @pl.when(step > 0)
    def _():
        pre[...] += pre_term
        back[...] += back_term

    @pl.when(step == steps - 1)
    def _():
        weight = meta_ref[:, 1:2]
        active, slope = gelu_pair(pre[...])
        grad = back[...]
        score = jnp.sum(active.astype(jnp.bfloat16).astype(jnp.float32) * grad, axis=1, keepdims=True)
        dw_ref[:rows] = (weight * grad * slope).astype(jnp.bfloat16)
        dw_ref[rows:] = (weight * active).astype(jnp.bfloat16)
        lg_ref[...] = jnp.broadcast_to(score * meta_ref[:, 2:3], lg_ref.shape)


def hidden(meta, t0, t1, g0, g1, w_up, w_down, dp):
    rows = meta.shape[0]
    tok_rows, width = t0.shape
    hid = w_up.shape[1]
    piece = width // dp
    block = pl.BlockSpec((tok_rows, piece), lambda k: (0, k))
    weight = pl.BlockSpec((piece, hid), lambda k: (k, 0))
    whole = lambda shape: pl.BlockSpec(shape, lambda k: (0, 0))
    return pl.pallas_call(
        hidden_kernel,
        grid=(dp,),
        in_specs=[whole(meta.shape), block, block, block, block, weight, weight],
        out_specs=[
            pl.BlockSpec((1, 2 * rows, piece), lambda k: (k, 0, 0)),
            whole((2 * rows, hid)),
            whole((rows, 128)),
        ],
        out_shape=[
            jax.ShapeDtypeStruct((dp, 2 * rows, piece), jnp.bfloat16),
            jax.ShapeDtypeStruct((2 * rows, hid), jnp.bfloat16),
            jax.ShapeDtypeStruct((rows, 128), jnp.float32),
        ],
        scratch_shapes=[pltpu.VMEM((rows, hid), jnp.float32)] * 2,
        compiler_params=pltpu.CompilerParams(vmem_limit_bytes=VMEM_LIMIT),
        cost_estimate=pl.CostEstimate(
            flops=4 * rows * width * hid, bytes_accessed=4 * width * hid + 8 * rows * width, transcendentals=rows * hid
        ),
        name="hidden",
    )(meta, t0, t1, g0, g1, w_up, w_down)


def rows_kernel(dw_ref, lg_ref, xg_ref, up_ref, router_ref, near_ref, far_ref, column_ref):
    rows = lg_ref.shape[0]
    half = rows // 2
    trailing = (((1,), (1,)), ((), ()))
    lg = lg_ref[:, 0:1]
    out = lax.dot_general(dw_ref[:rows], up_ref[...], trailing, preferred_element_type=jnp.float32)
    out = (out + lg * router_ref[...]).astype(jnp.bfloat16)
    near_ref[...] = out[:half]
    far_ref[...] = out[half:]
    column_ref[...] = jnp.sum(xg_ref[0].astype(jnp.float32) * lg, axis=0, keepdims=True)


def back_rows(dw, lg, xg, w_up, router_row):
    dp, double, piece = xg.shape
    rows = double // 2
    width, hid = w_up.shape
    whole = lambda shape: pl.BlockSpec(shape, lambda k: (0, 0))
    return pl.pallas_call(
        rows_kernel,
        grid=(dp,),
        in_specs=[
            whole(dw.shape),
            whole(lg.shape),
            pl.BlockSpec((1, rows, piece), lambda k: (k, 0, 0)),
            pl.BlockSpec((piece, hid), lambda k: (k, 0)),
            pl.BlockSpec((1, piece), lambda k: (0, k)),
        ],
        out_specs=[
            pl.BlockSpec((rows // 2, piece), lambda k: (0, k)),
            pl.BlockSpec((rows // 2, piece), lambda k: (0, k)),
            pl.BlockSpec((1, piece), lambda k: (0, k)),
        ],
        out_shape=[
            jax.ShapeDtypeStruct((rows // 2, width), jnp.bfloat16),
            jax.ShapeDtypeStruct((rows // 2, width), jnp.bfloat16),
            jax.ShapeDtypeStruct((1, width), jnp.float32),
        ],
        compiler_params=pltpu.CompilerParams(vmem_limit_bytes=VMEM_LIMIT),
        cost_estimate=pl.CostEstimate(
            flops=2 * rows * width * hid, bytes_accessed=2 * width * hid + 4 * rows * width, transcendentals=0
        ),
        name="back_rows",
    )(dw, lg, xg, w_up, router_row)


def weights_kernel(chunks, dp, has_start, has_end, place_ref, *refs):
    refs = list(refs)
    xgs = [refs.pop(0) for _ in range(chunks)]
    dws = [[refs.pop(0) for _ in range(dp)] for _ in range(chunks)]
    start = [refs.pop(0) for _ in range(2)] if has_start else None
    up_out, down_out = refs
    contract = (((0,), (0,)), ((), ()))
    place = place_ref[0]
    for which, out_ref in enumerate((up_out, down_out)):
        total = start[which][...] if has_start else None
        for chunk in range(chunks):
            rows = dws[chunk][0].shape[0] // 2
            left = jnp.concatenate(
                [xgs[chunk][place ^ k, which * rows : (which + 1) * rows] for k in range(dp)], axis=0
            )
            right = jnp.concatenate(
                [dws[chunk][k][which * rows : (which + 1) * rows] for k in range(dp)], axis=0
            )
            term = lax.dot_general(left, right, contract, preferred_element_type=jnp.float32)
            total = term if total is None else total + term
        out_ref[...] = total.astype(out_ref.dtype)


def weight_terms(place, xgs, dws, start, last):
    dp, double, piece = xgs[0].shape
    hid = dws[0][0].shape[1]
    tile = min(piece, 256)
    kind = jnp.bfloat16 if last else jnp.float32
    whole = pl.BlockSpec((double, hid), lambda i, place: (0, 0))
    strip = pl.BlockSpec((tile, hid), lambda i, place: (i, 0))
    flat = [block for group in dws for block in group]
    starts = list(start) if start is not None else []
    return pl.pallas_call(
        functools.partial(weights_kernel, len(xgs), dp, start is not None, last),
        grid_spec=pltpu.PrefetchScalarGridSpec(
            num_scalar_prefetch=1,
            grid=(piece // tile,),
            in_specs=[pl.BlockSpec((dp, double, tile), lambda i, place: (0, 0, i))] * len(xgs)
            + [whole] * len(flat)
            + [strip] * len(starts),
            out_specs=[strip, strip],
        ),
        out_shape=[jax.ShapeDtypeStruct((piece, hid), kind)] * 2,
        compiler_params=pltpu.CompilerParams(vmem_limit_bytes=VMEM_LIMIT),
        cost_estimate=pl.CostEstimate(
            flops=2 * len(xgs) * dp * double * piece * hid,
            bytes_accessed=2 * len(xgs) * dp * double * (piece + hid) + 8 * piece * hid,
            transcendentals=0,
        ),
        name="weight_terms",
    )(place, *xgs, *flat, *starts)


def combine_kernel(slots_ref, *refs):
    blocks, out_ref = refs[:-1], refs[-1]
    tok_rows = out_ref.shape[0]
    places = lax.broadcasted_iota(jnp.int32, (tok_rows, slots_ref.shape[1]), 0).astype(jnp.float32)
    picks = jnp.where(slots_ref[...] == places, 1.0, 0.0).astype(jnp.bfloat16)
    rows = jnp.concatenate([block[...] for block in blocks], axis=0)
    out_ref[...] = jnp.dot(picks, rows, preferred_element_type=jnp.float32).astype(out_ref.dtype)


def combine(slots, blocks, tok_rows):
    per_slot, width = blocks[0].shape
    tile = 1024 if width % 1024 == 0 else width
    block = pl.BlockSpec((per_slot, tile), lambda k: (0, k))
    return pl.pallas_call(
        combine_kernel,
        grid=(width // tile,),
        in_specs=[pl.BlockSpec(slots.shape, lambda k: (0, 0))] + [block] * len(blocks),
        out_specs=pl.BlockSpec((tok_rows, tile), lambda k: (0, k)),
        out_shape=jax.ShapeDtypeStruct((tok_rows, width), jnp.bfloat16),
        compiler_params=pltpu.CompilerParams(vmem_limit_bytes=VMEM_LIMIT),
        cost_estimate=pl.CostEstimate(
            flops=2 * len(blocks) * per_slot * tok_rows * width,
            bytes_accessed=2 * len(blocks) * per_slot * width,
            transcendentals=0,
        ),
        name="combine",
    )(slots, *blocks)


def on_line(tokens, out_grad, route_slots, expert_counts, router_weight, up_weight, down_weight):
    experts = lax.axis_size("expert")
    dp = lax.axis_size("dp")
    chips = experts // 2
    me = lax.axis_index("expert")
    place = lax.axis_index("dp")
    chip = me // 2
    core = me % 2
    tok_rows = tokens.shape[0]
    slots = route_slots[0, 0]
    per_slot = slots.shape[1]
    w_up = up_weight[0]
    w_down = down_weight[0]
    everyone = range(experts)

    def along(block, step):
        pairs = [(e, e + 2 * step) for e in everyone if 0 <= e + 2 * step < experts]
        return lax.ppermute(block, "expert", pairs)

    def across(block, mask):
        return lax.ppermute(block, "expert", [(e, e ^ mask) for e in everyone])

    right, left = [(tokens, out_grad)], [(tokens, out_grad)]
    for _ in range(chips - 1):
        t_right, t_left = along(right[-1][0], 1), along(left[-1][0], -1)
        g_right, g_left = along(right[-1][1], 1), along(left[-1][1], -1)
        right.append((t_right, g_right))
        left.append((t_left, g_left))

    gates = jax.nn.sigmoid(gate_logits(tokens, router_weight)).T
    counts = jnp.maximum(expert_counts, 1).astype(jnp.float32)[None, :]
    weights = gates / counts
    slopes = gates * (1.0 - gates) / counts
    slots_float = slots.astype(jnp.float32)
    facts = lax.all_to_all(
        jnp.concatenate([slots_float, weights, slopes], axis=1), "expert", 0, 0, tiled=True
    )
    got_slots = facts[:, :per_slot]
    hits = got_slots[:, :, None] == jnp.arange(tok_rows, dtype=jnp.float32)[None, None, :]
    got_weights = jnp.sum(jnp.where(hits, facts[:, None, per_slot : per_slot + tok_rows], 0.0), axis=2)
    got_slopes = jnp.sum(jnp.where(hits, facts[:, None, per_slot + tok_rows :], 0.0), axis=2)
    metas = jnp.stack([got_slots, got_weights, got_slopes], axis=-1).reshape(chips, 2, per_slot, 3)
    metas = jnp.where(core == 0, metas, metas[:, ::-1]).reshape(chips, 2 * per_slot, 3)
    mine = slots_float.reshape(chips, 2, per_slot)
    mine = jnp.where(core == 0, mine, mine[:, ::-1])
    order = [chip ^ j for j in range(chips)]
    mine = jnp.concatenate([lax.dynamic_index_in_dim(mine, k, 0, False) for k in order], axis=0)

    router_row = lax.dynamic_index_in_dim(router_weight.T, me, 0, True)
    place_array = jnp.reshape(place, (1,)).astype(jnp.int32)

    def source(j, which):
        if j == 0:
            return right[0][which]
        result = None
        for here in range(chips):
            other = here ^ j
            block = left[other - here][which] if other > here else right[here - other][which]
            result = block if result is None else jnp.where(chip == here, block, result)
        return result

    xgs, dws, blocks, columns = [], [], [], []
    for j in range(chips):
        t_near, g_near = source(j, 0), source(j, 1)
        t_far, g_far = across(t_near, 1), across(g_near, 1)
        meta = lax.dynamic_index_in_dim(metas, order[j], 0, False)
        xg, dw, lg = hidden(meta, t_near, t_far, g_near, g_far, w_up, w_down, dp)
        xgs.append(lax.all_to_all(xg, "dp", 0, 0, tiled=True))
        dws.append(
            [dw] + [lax.ppermute(dw, "dp", [(q, q ^ k) for q in range(dp)]) for k in range(1, dp)]
        )
        near, far, column = back_rows(dw, lg, xg, w_up, router_row)
        blocks.append(near if j == 0 else across(near, 2 * j))
        blocks.append(across(far, 2 * j + 1))
        columns.append(column)

    early = weight_terms(place_array, xgs[:-1], dws[:-1], None, False)
    up_sum, down_sum = weight_terms(place_array, xgs[-1:], dws[-1:], early, True)
    tokens_grad = combine(mine.reshape(1, -1), blocks, tok_rows)
    router_grad = lax.psum(sum(columns), "dp").T
    return (tokens_grad, up_sum[None], down_sum[None], router_grad)


def on_any(tokens, out_grad, route_slots, expert_counts, router_weight, up_weight, down_weight):
    experts = lax.axis_size("expert")
    me = lax.axis_index("expert")
    tok_rows = tokens.shape[0]
    width = tokens.shape[1]
    slots = route_slots[0, 0]
    per_slot = slots.shape[1]
    received = experts * per_slot
    contract = (((0,), (0,)), ((), ()))
    trailing = (((1,), (1,)), ((), ()))
    picks = slots[:, :, None] == jnp.arange(tok_rows, dtype=jnp.int32)[None, None, :]
    pick_half = picks.astype(jnp.bfloat16).reshape(received, tok_rows)
    gates = jax.nn.sigmoid(gate_logits(tokens, router_weight)).T
    counts = jnp.maximum(expert_counts, 1).astype(jnp.float32)[None, :]
    weight_slot = jnp.sum(jnp.where(picks, (gates / counts)[:, None, :], 0.0), axis=2)
    slope_slot = jnp.sum(jnp.where(picks, (gates * (1.0 - gates) / counts)[:, None, :], 0.0), axis=2)
    swap = lambda block: lax.all_to_all(block, "expert", split_axis=0, concat_axis=0, tiled=True)
    send_rows = jnp.dot(pick_half, tokens, preferred_element_type=jnp.float32).astype(jnp.bfloat16)
    send_grads = jnp.dot(pick_half, out_grad, preferred_element_type=jnp.float32).astype(jnp.bfloat16)
    rows_in = swap(send_rows)
    grads_in = swap(send_grads)
    facts = swap(jnp.concatenate([weight_slot, slope_slot], axis=1))
    weight_in = facts[:, :per_slot].reshape(received)
    slope_in = facts[:, per_slot:].reshape(received)
    w_up = up_weight[0]
    w_down = down_weight[0]
    pre = jnp.dot(rows_in, w_up, preferred_element_type=jnp.float32)
    active, slope = gelu_pair(pre)
    grad = jnp.dot(grads_in, w_down, preferred_element_type=jnp.float32)
    score = jnp.sum(active.astype(jnp.bfloat16).astype(jnp.float32) * grad, axis=1)
    logit_grad = score * slope_in
    pre_grad = (weight_in[:, None] * grad * slope).astype(jnp.bfloat16)
    scaled = (weight_in[:, None] * active).astype(jnp.bfloat16)
    router_row = lax.dynamic_index_in_dim(router_weight.T, me, 0, True)
    row_grad = lax.dot_general(pre_grad, w_up, trailing, preferred_element_type=jnp.float32)
    back = swap((row_grad + logit_grad[:, None] * router_row).astype(jnp.bfloat16))
    up_term = lax.dot_general(rows_in, pre_grad, contract, preferred_element_type=jnp.float32)
    down_term = lax.dot_general(grads_in, scaled, contract, preferred_element_type=jnp.float32)
    spread = lambda term: lax.psum_scatter(
        term.astype(jnp.bfloat16), "dp", scatter_dimension=0, tiled=True
    )
    tokens_grad = lax.dot_general(pick_half, back, contract, preferred_element_type=jnp.float32)
    column = jnp.sum(logit_grad[:, None] * rows_in.astype(jnp.float32), axis=0, keepdims=True)
    router_grad = lax.psum(column, "dp").T
    return (tokens_grad.astype(jnp.bfloat16), spread(up_term)[None], spread(down_term)[None], router_grad)


def solution(mesh):
    line = mesh.shape["expert"] == 8 and mesh.shape["dp"] == 4
    return jax.shard_map(
        on_line if line else on_any,
        mesh=mesh,
        in_specs=(
            P(("dp", "expert"), None),
            P(("dp", "expert"), None),
            P("dp", "expert", None, None),
            P(("dp", "expert")),
            P(),
            P("expert", None, None),
            P("expert", None, None),
        ),
        out_specs=(
            P(("dp", "expert"), None),
            P("expert", "dp", None),
            P("expert", "dp", None),
            P(None, "expert"),
        ),
        check_vma=False,
    )
```

```python
import functools

import jax
import jax.numpy as jnp
from jax import lax
from jax.experimental import pallas as pl
from jax.experimental.pallas import tpu as pltpu
from jax.sharding import PartitionSpec as P

SPLIT = True
VMEM_LIMIT = 48 * 1024 * 1024
SMALL = pl.CostEstimate(flops=1024, bytes_accessed=1024, transcendentals=0)


def gelu_pair(values):
    inner = 0.7978845608 * (values + 0.044715 * values * values * values)
    tangent = jnp.tanh(inner)
    result = 0.5 * values * (1.0 + tangent)
    slope = 0.5 * (1.0 + tangent) + 0.5 * values * (1.0 - tangent * tangent) * 0.7978845608 * (
        1.0 + 3.0 * 0.044715 * values * values
    )
    return (result, slope)


def gate_logits(tokens, router_weight):
    high = lax.reduce_precision(router_weight, 8, 7)
    rest = router_weight - high
    middle = lax.reduce_precision(rest, 8, 7)
    low = rest - middle
    terms = jnp.concatenate([high, middle, low], axis=1).astype(jnp.bfloat16)
    parts = jnp.dot(tokens, terms, preferred_element_type=jnp.float32)
    experts = router_weight.shape[1]
    return parts[:, :experts] + parts[:, experts : 2 * experts] + parts[:, 2 * experts :]


EXTRA = 16


LARGE = pl.CostEstimate(flops=10000000000, bytes_accessed=1024, transcendentals=0)


def picks_of(meta_ref, tok_rows):
    places = lax.broadcasted_iota(jnp.int32, (meta_ref.shape[0], tok_rows), 1).astype(jnp.float32)
    return jnp.where(meta_ref[:, 0:1] == places, 1.0, 0.0).astype(jnp.bfloat16)


def pick(picks, near_ref, far_ref, first):
    half = picks.shape[0] // 2
    part = pl.ds(first, picks.shape[1])
    top = jnp.dot(picks[:half], near_ref[part], preferred_element_type=jnp.float32)
    bottom = jnp.dot(picks[half:], far_ref[part], preferred_element_type=jnp.float32)
    return jnp.concatenate([top, bottom], axis=0).astype(jnp.bfloat16)


def pick_kernel(meta_ref, near_ref, far_ref, out_ref):
    rows = meta_ref.shape[0]
    tok_rows = near_ref.shape[0] // 2
    picks = picks_of(meta_ref, tok_rows)
    out_ref[0, :rows] = pick(picks, near_ref, far_ref, 0)
    out_ref[0, rows:] = pick(picks, near_ref, far_ref, tok_rows)


def pick_rows(meta, near, far, dp):
    rows = meta.shape[0]
    both_rows, width = near.shape
    piece = width // dp
    block = pl.BlockSpec((both_rows, piece), lambda k: (0, k))
    return pl.pallas_call(
        pick_kernel,
        grid=(dp,),
        in_specs=[pl.BlockSpec(meta.shape, lambda k: (0, 0)), block, block],
        out_specs=pl.BlockSpec((1, 2 * rows, piece), lambda k: (k, 0, 0)),
        out_shape=jax.ShapeDtypeStruct((dp, 2 * rows, piece), jnp.bfloat16),
        compiler_params=pltpu.CompilerParams(vmem_limit_bytes=VMEM_LIMIT),
        cost_estimate=SMALL,
        name="pick_rows",
    )(meta, near, far)


def hidden_kernel(ready, meta_ref, router_ref, *refs):
    sources, refs = (refs[:1], refs[1:]) if ready else (refs[:2], refs[2:])
    up_ref, down_ref, message_ref, lg_ref, pre, back, logit, held = refs
    step = pl.program_id(0)
    steps = pl.num_programs(0)
    rows = meta_ref.shape[0]
    trailing = (((1,), (1,)), ((), ()))
    if ready:
        x, g = sources[0][0, :rows], sources[0][0, rows:]
    else:
        tok_rows = sources[0].shape[0] // 2
        picks = picks_of(meta_ref, tok_rows)
        x, g = pick(picks, *sources, 0), pick(picks, *sources, tok_rows)
        message_ref[step, :rows] = x
        message_ref[step, rows : 2 * rows] = g
    held[step] = x
    pre_term = jnp.dot(x, up_ref[...], preferred_element_type=jnp.float32)
    back_term = jnp.dot(g, down_ref[...], preferred_element_type=jnp.float32)
    logit_term = lax.dot_general(x, router_ref[...], trailing, preferred_element_type=jnp.float32)

    @pl.when(step == 0)
    def _():
        pre[...] = pre_term
        back[...] = back_term
        logit[...] = logit_term

    @pl.when(step > 0)
    def _():
        pre[...] += pre_term
        back[...] += back_term
        logit[...] += logit_term

    @pl.when(step == steps - 1)
    def _():
        gate = jax.nn.sigmoid(jnp.sum(logit[...], axis=1, keepdims=True))
        weight = gate * meta_ref[:, 1:2]
        active, slope = gelu_pair(pre[...])
        grad = back[...]
        score = jnp.sum(active.astype(jnp.bfloat16).astype(jnp.float32) * grad, axis=1, keepdims=True)
        pre_grad = (weight * grad * slope).astype(jnp.bfloat16)
        scaled = (weight * active).astype(jnp.bfloat16)
        lg = score * weight * (1.0 - gate)
        lg_ref[...] = jnp.broadcast_to(lg, lg_ref.shape)
        flat = jnp.transpose(jnp.broadcast_to(lg, (rows, rows)))[:8]
        high = flat.astype(jnp.bfloat16)
        rest = flat - high.astype(jnp.float32)
        middle = rest.astype(jnp.bfloat16)
        low = (rest - middle.astype(jnp.float32)).astype(jnp.bfloat16)
        columns = []
        for k in range(held.shape[0]):
            terms = [jnp.dot(part, held[k], preferred_element_type=jnp.float32) for part in (high, middle, low)]
            columns.append((terms[0] + terms[1] + terms[2])[0:1])
        column = jnp.concatenate(columns, axis=0)
        first = column.astype(jnp.bfloat16)
        second = (column - first.astype(jnp.float32)).astype(jnp.bfloat16)
        empty = jnp.zeros((EXTRA - 2 * column.shape[0], column.shape[1]), jnp.float32)
        extra = jnp.concatenate(
            [first.astype(jnp.float32), second.astype(jnp.float32), empty], axis=0
        ).astype(jnp.bfloat16)
        base = 0 if ready else 2 * rows
        for k in range(message_ref.shape[0]):
            message_ref[k, base : base + rows] = pre_grad
            message_ref[k, base + rows : base + 2 * rows] = scaled
            message_ref[k, base + 2 * rows :] = extra


def hidden(meta, router, sources, w_up, w_down, dp):
    rows = meta.shape[0]
    width, hid = w_up.shape
    piece = width // dp
    ready = len(sources) == 1
    shape = (1, 2 * rows + EXTRA, piece) if ready else (dp, 4 * rows + EXTRA, piece)
    weight = pl.BlockSpec((piece, hid), lambda k: (k, 0))
    whole = lambda shape: pl.BlockSpec(shape, lambda k: (0,) * len(shape))
    if ready:
        blocks = [pl.BlockSpec((1, 2 * rows, piece), lambda k: (k, 0, 0))]
    else:
        blocks = [pl.BlockSpec((sources[0].shape[0], piece), lambda k: (0, k))] * 2
    return pl.pallas_call(
        functools.partial(hidden_kernel, ready),
        grid=(dp,),
        in_specs=[whole(meta.shape), pl.BlockSpec((router.shape[0], piece), lambda k: (0, k))]
        + blocks
        + [weight, weight],
        out_specs=[whole(shape), whole((rows, 128))],
        out_shape=[
            jax.ShapeDtypeStruct(shape, jnp.bfloat16),
            jax.ShapeDtypeStruct((rows, 128), jnp.float32),
        ],
        scratch_shapes=[pltpu.VMEM((rows, hid), jnp.float32)] * 2
        + [pltpu.VMEM((rows, router.shape[0]), jnp.float32), pltpu.VMEM((dp, rows, piece), jnp.bfloat16)],
        compiler_params=pltpu.CompilerParams(vmem_limit_bytes=VMEM_LIMIT),
        cost_estimate=SMALL,
        name="hidden",
    )(meta, router, *sources, w_up, w_down)


def rows_kernel(grad_ref, lg_ref, up_ref, router_ref, near_ref, far_ref):
    rows = lg_ref.shape[0]
    half = rows // 2
    trailing = (((1,), (1,)), ((), ()))
    out = lax.dot_general(grad_ref[...].reshape(rows, -1), up_ref[...], trailing, preferred_element_type=jnp.float32)
    out = (out + lg_ref[:, 0:1] * router_ref[...]).astype(jnp.bfloat16)
    near_ref[...] = out[:half]
    far_ref[...] = out[half:]


def back_rows(message, lg, w_up, router_row, steps):
    first = 0 if message.shape[0] == 1 else 2
    rows = lg.shape[0]
    width, hid = w_up.shape
    piece = width // steps
    whole = lambda shape: pl.BlockSpec(shape, lambda k: (0, 0))
    half = pl.BlockSpec((rows // 2, piece), lambda k: (0, k))
    return pl.pallas_call(
        rows_kernel,
        grid=(steps,),
        in_specs=[
            pl.BlockSpec((1, rows, hid), lambda k: (0, first, 0)),
            whole(lg.shape),
            pl.BlockSpec((piece, hid), lambda k: (k, 0)),
            pl.BlockSpec((1, piece), lambda k: (0, k)),
        ],
        out_specs=[half, half],
        out_shape=[jax.ShapeDtypeStruct((rows // 2, width), jnp.bfloat16)] * 2,
        compiler_params=pltpu.CompilerParams(vmem_limit_bytes=VMEM_LIMIT),
        cost_estimate=SMALL,
        name="back_rows",
    )(message, lg, w_up, router_row)


def weights_kernel(sizes, has_start, place_ref, *refs):
    refs = list(refs)
    chunks = []
    for size in sizes:
        left = refs.pop(0)
        dp, double = left.shape[:2]
        rows = double // 2
        rights = [refs.pop(0) for _ in range(size)]
        if size == 1:
            pairs = [(left.at[k], rights[0].at[k], 2 * rows) for k in range(dp)]
        else:
            pairs = [(left.at[place_ref[0] ^ k], rights[k].at[0], 0) for k in range(dp)]
        chunks.append(pairs)
    start = [refs.pop(0) for _ in range(3)] if has_start else None
    outs = refs
    contract = (((0,), (0,)), ((), ()))
    for which in range(2):
        total = start[which][...] if has_start else None
        low = which * rows
        for pairs in chunks:
            left = jnp.concatenate([ref[low : low + rows] for ref, _, _ in pairs], axis=0)
            right = jnp.concatenate([ref[base + low : base + low + rows] for _, ref, base in pairs], axis=0)
            term = lax.dot_general(left, right, contract, preferred_element_type=jnp.float32)
            total = term if total is None else total + term
        outs[which][...] = total.astype(outs[which].dtype)
    column = start[2][...] if has_start else jnp.zeros(outs[2].shape, jnp.float32)
    for pairs in chunks:
        for _, ref, base in pairs:
            both = ref[base + 2 * rows :].astype(jnp.float32)
            column = column + both[:dp] + both[dp : 2 * dp]
    outs[2][...] = column


def weight_terms(place, chunks, rows, start, last):
    dp, _, piece = chunks[0][0].shape
    tile = min(piece, 256)
    kind = jnp.bfloat16 if last else jnp.float32
    strip = pl.BlockSpec((tile, piece), lambda i, place: (i, 0))
    column = pl.BlockSpec((dp, piece), lambda i, place: (0, 0))
    specs, arrays = [], []
    for blocks in chunks:
        rights = blocks if len(blocks) == 1 else blocks[1:]
        specs.append(pl.BlockSpec((dp, 2 * rows, tile), lambda i, place: (0, 0, i)))
        specs += [pl.BlockSpec(block.shape, lambda i, place: (0, 0, 0)) for block in rights]
        arrays += [blocks[0], *rights]
    if start is not None:
        specs += [strip, strip, column]
        arrays += list(start)
    sizes = [1 if len(blocks) == 1 else len(blocks) - 1 for blocks in chunks]
    return pl.pallas_call(
        functools.partial(weights_kernel, sizes, start is not None),
        grid_spec=pltpu.PrefetchScalarGridSpec(
            num_scalar_prefetch=1, grid=(piece // tile,), in_specs=specs, out_specs=[strip, strip, column]
        ),
        out_shape=[jax.ShapeDtypeStruct((piece, piece), kind)] * 2
        + [jax.ShapeDtypeStruct((dp, piece), jnp.float32)],
        compiler_params=pltpu.CompilerParams(vmem_limit_bytes=VMEM_LIMIT),
        cost_estimate=SMALL if last else LARGE,
        name="weight_terms",
    )(place, *arrays)


def combine_kernel(slots_ref, *refs):
    blocks, out_ref = refs[:-1], refs[-1]
    tok_rows = out_ref.shape[0]
    places = lax.broadcasted_iota(jnp.int32, (tok_rows, slots_ref.shape[1]), 0).astype(jnp.float32)
    picks = jnp.where(slots_ref[...] == places, 1.0, 0.0).astype(jnp.bfloat16)
    rows = jnp.concatenate([block[...] for block in blocks], axis=0)
    out_ref[...] = jnp.dot(picks, rows, preferred_element_type=jnp.float32).astype(out_ref.dtype)


def combine(slots, blocks, tok_rows):
    per_slot, width = blocks[0].shape
    tile = 1024 if width % 1024 == 0 else width
    block = pl.BlockSpec((per_slot, tile), lambda k: (0, k))
    return pl.pallas_call(
        combine_kernel,
        grid=(width // tile,),
        in_specs=[pl.BlockSpec(slots.shape, lambda k: (0, 0))] + [block] * len(blocks),
        out_specs=pl.BlockSpec((tok_rows, tile), lambda k: (0, k)),
        out_shape=jax.ShapeDtypeStruct((tok_rows, width), jnp.bfloat16),
        compiler_params=pltpu.CompilerParams(vmem_limit_bytes=VMEM_LIMIT),
        cost_estimate=SMALL,
        name="combine",
    )(slots, *blocks)


def after(block, *others):
    return lax.optimization_barrier((block,) + others)[0]


def on_line(tokens, out_grad, route_slots, expert_counts, router_weight, up_weight, down_weight):
    experts = lax.axis_size("expert")
    dp = lax.axis_size("dp")
    chips = experts // 2
    me = lax.axis_index("expert")
    chip = me // 2
    core = me % 2
    tok_rows = tokens.shape[0]
    slots = route_slots[0, 0]
    per_slot = slots.shape[1]
    w_up = up_weight[0]
    w_down = down_weight[0]
    middle = jnp.logical_and(chip >= 1, chip <= 2)

    def between(block, chip_pairs):
        pairs = [(2 * a + c, 2 * b + c) for a, b in chip_pairs for c in range(2)]
        return lax.ppermute(block, "expert", pairs)

    def across(block, mask):
        return lax.ppermute(block, "expert", [(e, e ^ mask) for e in range(experts)])

    slots_float = slots.astype(jnp.float32)
    counts = jnp.broadcast_to(expert_counts.astype(jnp.float32)[None, :], (experts, tok_rows))
    own_facts = jnp.concatenate([slots_float, counts], axis=1)
    facts = lax.all_to_all(own_facts, "expert", 0, 0, tiled=True)
    got_slots = facts[:, :per_slot]
    hits = got_slots[:, :, None] == jnp.arange(tok_rows, dtype=jnp.float32)[None, None, :]
    got_counts = jnp.sum(jnp.where(hits, facts[:, None, per_slot:], 0.0), axis=2)
    shares = jnp.where(got_slots >= 0, 1.0 / jnp.maximum(got_counts, 1.0), 0.0)
    metas = jnp.stack([got_slots, shares], axis=-1).reshape(chips, 2, per_slot, 2)
    metas = jnp.where(core == 0, metas, metas[:, ::-1]).reshape(chips, 2 * per_slot, 2)
    mine = slots_float.reshape(chips, 2, per_slot)
    mine = jnp.where(core == 0, mine, mine[:, ::-1])
    order = [chip ^ j for j in range(chips)]
    mine = jnp.concatenate([lax.dynamic_index_in_dim(mine, k, 0, False) for k in order], axis=0)

    router_row = lax.dynamic_index_in_dim(router_weight.T, me, 0, True)
    high = lax.reduce_precision(router_row, 8, 7)
    rest = router_row - high
    mid = lax.reduce_precision(rest, 8, 7)
    router = jnp.concatenate([high, mid, rest - mid, jnp.zeros((13, high.shape[1]), jnp.float32)], axis=0)
    router = router.astype(jnp.bfloat16)

    ends = [(0, 1), (1, 0), (2, 3), (3, 2)]
    inner = [(1, 2), (2, 1)]
    outward = [(1, 0), (2, 3)]

    def settle(pair):
        return pair if not isinstance(pair, tuple) else jnp.where(middle, pair[0], pair[1])

    own = after(jnp.concatenate([tokens, out_grad], axis=0), facts)
    one, inside = between(own, ends), between(own, inner)

    place = jnp.reshape(lax.axis_index("dp"), (1,)).astype(jnp.int32)

    def exchange(block):
        return lax.all_to_all(block, "dp", 0, 0, tiled=True)

    def chunk(j, pair, before, split=False):
        near_block = settle(pair)
        far_block = across(near_block, 1)
        meta = lax.dynamic_index_in_dim(metas, order[j], 0, False)
        meta = after(meta, *before)
        if split:
            rows = pick_rows(meta, near_block, far_block, dp)
            message, lg = hidden(meta, router, (rows,), w_up, w_down, dp)
            got = [exchange(rows), message]
            for k in range(1, dp):
                got.append(lax.ppermute(message, "dp", [(q, q ^ k) for q in range(dp)]))
        else:
            message, lg = hidden(meta, router, (near_block, far_block), w_up, w_down, dp)
            got = [exchange(message)]
        near, far = back_rows(message, lg, w_up, router_row, dp)
        return got, jnp.concatenate([near, across(far, 1)], axis=0)

    got0, back0 = chunk(0, own, ())
    inside_two, out_two = between(one, inner), between(inside, outward)
    got1, back1 = chunk(1, one, (back0,))
    out_three = between(inside_two, outward)
    got2, back2 = chunk(2, (inside_two, out_two), (back1,))
    got3, back3 = chunk(3, (inside, out_three), (back2,), split=SPLIT)
    back1, back2 = across(back1, 2), across(back2, 4)
    back3 = across(after(back3, back1, back2), 6)
    rows = 2 * per_slot
    early = weight_terms(place, [got0, got1, got2], rows, None, False)
    blocks = [back0, back1, back2, back3]
    up_sum, down_sum, column = weight_terms(place, [got3], rows, early, True)
    tokens_grad = combine(mine.reshape(1, -1), blocks, tok_rows)
    return (tokens_grad, up_sum[None], down_sum[None], column.reshape(-1, 1))


def on_any(tokens, out_grad, route_slots, expert_counts, router_weight, up_weight, down_weight):
    experts = lax.axis_size("expert")
    me = lax.axis_index("expert")
    tok_rows = tokens.shape[0]
    width = tokens.shape[1]
    slots = route_slots[0, 0]
    per_slot = slots.shape[1]
    received = experts * per_slot
    contract = (((0,), (0,)), ((), ()))
    trailing = (((1,), (1,)), ((), ()))
    picks = slots[:, :, None] == jnp.arange(tok_rows, dtype=jnp.int32)[None, None, :]
    pick_half = picks.astype(jnp.bfloat16).reshape(received, tok_rows)
    gates = jax.nn.sigmoid(gate_logits(tokens, router_weight)).T
    counts = jnp.maximum(expert_counts, 1).astype(jnp.float32)[None, :]
    weight_slot = jnp.sum(jnp.where(picks, (gates / counts)[:, None, :], 0.0), axis=2)
    slope_slot = jnp.sum(jnp.where(picks, (gates * (1.0 - gates) / counts)[:, None, :], 0.0), axis=2)
    swap = lambda block: lax.all_to_all(block, "expert", split_axis=0, concat_axis=0, tiled=True)
    send_rows = jnp.dot(pick_half, tokens, preferred_element_type=jnp.float32).astype(jnp.bfloat16)
    send_grads = jnp.dot(pick_half, out_grad, preferred_element_type=jnp.float32).astype(jnp.bfloat16)
    rows_in = swap(send_rows)
    grads_in = swap(send_grads)
    facts = swap(jnp.concatenate([weight_slot, slope_slot], axis=1))
    weight_in = facts[:, :per_slot].reshape(received)
    slope_in = facts[:, per_slot:].reshape(received)
    w_up = up_weight[0]
    w_down = down_weight[0]
    pre = jnp.dot(rows_in, w_up, preferred_element_type=jnp.float32)
    active, slope = gelu_pair(pre)
    grad = jnp.dot(grads_in, w_down, preferred_element_type=jnp.float32)
    score = jnp.sum(active.astype(jnp.bfloat16).astype(jnp.float32) * grad, axis=1)
    logit_grad = score * slope_in
    pre_grad = (weight_in[:, None] * grad * slope).astype(jnp.bfloat16)
    scaled = (weight_in[:, None] * active).astype(jnp.bfloat16)
    router_row = lax.dynamic_index_in_dim(router_weight.T, me, 0, True)
    row_grad = lax.dot_general(pre_grad, w_up, trailing, preferred_element_type=jnp.float32)
    back = swap((row_grad + logit_grad[:, None] * router_row).astype(jnp.bfloat16))
    up_term = lax.dot_general(rows_in, pre_grad, contract, preferred_element_type=jnp.float32)
    down_term = lax.dot_general(grads_in, scaled, contract, preferred_element_type=jnp.float32)
    spread = lambda term: lax.psum_scatter(
        term.astype(jnp.bfloat16), "dp", scatter_dimension=0, tiled=True
    )
    tokens_grad = lax.dot_general(pick_half, back, contract, preferred_element_type=jnp.float32)
    column = jnp.sum(logit_grad[:, None] * rows_in.astype(jnp.float32), axis=0, keepdims=True)
    router_grad = lax.psum(column, "dp").T
    return (tokens_grad.astype(jnp.bfloat16), spread(up_term)[None], spread(down_term)[None], router_grad)


def solution(mesh):
    line = mesh.shape["expert"] == 8 and mesh.shape["dp"] == 4
    return jax.shard_map(
        on_line if line else on_any,
        mesh=mesh,
        in_specs=(
            P(("dp", "expert"), None),
            P(("dp", "expert"), None),
            P("dp", "expert", None, None),
            P(("dp", "expert")),
            P(),
            P("expert", None, None),
            P("expert", None, None),
        ),
        out_specs=(
            P(("dp", "expert"), None),
            P("expert", "dp", None),
            P("expert", "dp", None),
            P(None, "expert"),
        ),
        check_vma=False,
    )
```

```python
import functools

import jax
import jax.numpy as jnp
from jax import lax
from jax.experimental import pallas as pl
from jax.experimental.pallas import tpu as pltpu
from jax.sharding import PartitionSpec as P

STRIP = 1024
VMEM_LIMIT = 56 * 1024 * 1024
SMALL = pl.CostEstimate(flops=1024, bytes_accessed=1024, transcendentals=0)


def gelu_pair(values):
    inner = 0.7978845608 * (values + 0.044715 * values * values * values)
    tangent = jnp.tanh(inner)
    result = 0.5 * values * (1.0 + tangent)
    slope = 0.5 * (1.0 + tangent) + 0.5 * values * (1.0 - tangent * tangent) * 0.7978845608 * (
        1.0 + 3.0 * 0.044715 * values * values
    )
    return (result, slope)


def gate_logits(tokens, router_weight):
    high = lax.reduce_precision(router_weight, 8, 7)
    rest = router_weight - high
    middle = lax.reduce_precision(rest, 8, 7)
    low = rest - middle
    terms = jnp.concatenate([high, middle, low], axis=1).astype(jnp.bfloat16)
    parts = jnp.dot(tokens, terms, preferred_element_type=jnp.float32)
    experts = router_weight.shape[1]
    return parts[:, :experts] + parts[:, experts : 2 * experts] + parts[:, 2 * experts :]


EXTRA = 16


LARGE = pl.CostEstimate(flops=10000000000, bytes_accessed=1024, transcendentals=0)


def picks_of(meta_ref, tok_rows):
    places = lax.broadcasted_iota(jnp.int32, (meta_ref.shape[0], tok_rows), 1).astype(jnp.float32)
    return jnp.where(meta_ref[:, 0:1] == places, 1.0, 0.0).astype(jnp.bfloat16)


def pick(picks, near_ref, far_ref, first):
    half = picks.shape[0] // 2
    part = pl.ds(first, picks.shape[1])
    top = jnp.dot(picks[:half], near_ref[part], preferred_element_type=jnp.float32)
    bottom = jnp.dot(picks[half:], far_ref[part], preferred_element_type=jnp.float32)
    return jnp.concatenate([top, bottom], axis=0).astype(jnp.bfloat16)


def expert_kernel(apart, steps, place_ref, meta_ref, router_ref, *refs):
    sources, (up_ref, down_ref, row_ref), messages = refs[:2], refs[2:5], refs[5:-8]
    near_ref, far_ref, pre, back, logit, held, held_up, lgs = refs[-8:]
    step = pl.program_id(0)
    rows = meta_ref.shape[0]
    half = rows // 2
    trailing = (((1,), (1,)), ((), ()))
    tok_rows = sources[0].shape[0] // 2
    dp, _, piece = held.shape
    strip = up_ref.shape[0]
    per_piece = piece // strip

    @pl.when(step < steps)
    def _():
        picks = picks_of(meta_ref, tok_rows)
        x, g = pick(picks, *sources, 0), pick(picks, *sources, tok_rows)
        shard = step // per_piece
        lanes = pl.ds(pl.multiple_of(step % per_piece * strip, strip), strip)
        if apart:
            for k, message_ref in enumerate(messages):

                @pl.when(shard ^ place_ref[0] == k)
                def _():
                    message_ref[0, :rows, lanes] = x
                    message_ref[0, rows : 2 * rows, lanes] = g
        else:
            messages[0][shard, :rows, lanes] = x
            messages[0][shard, rows : 2 * rows, lanes] = g
        held[shard, :, lanes] = x
        held_up[step] = up_ref[...]
        pre_term = jnp.dot(x, up_ref[...], preferred_element_type=jnp.float32)
        back_term = jnp.dot(g, down_ref[...], preferred_element_type=jnp.float32)
        logit_term = lax.dot_general(x, router_ref[...], trailing, preferred_element_type=jnp.float32)

        @pl.when(step == 0)
        def _():
            pre[...] = pre_term
            back[...] = back_term
            logit[...] = logit_term

        @pl.when(step > 0)
        def _():
            pre[...] += pre_term
            back[...] += back_term
            logit[...] += logit_term

    @pl.when(step == steps - 1)
    def _():
        gate = jax.nn.sigmoid(jnp.sum(logit[...], axis=1, keepdims=True))
        weight = gate * meta_ref[:, 1:2]
        active, slope = gelu_pair(pre[...])
        grad = back[...]
        score = jnp.sum(active.astype(jnp.bfloat16).astype(jnp.float32) * grad, axis=1, keepdims=True)
        pre_grad = (weight * grad * slope).astype(jnp.bfloat16)
        scaled = (weight * active).astype(jnp.bfloat16)
        lg = score * weight * (1.0 - gate)
        lgs[...] = jnp.broadcast_to(lg, lgs.shape)
        flat = jnp.transpose(jnp.broadcast_to(lg, (rows, rows)))[:8]
        high = flat.astype(jnp.bfloat16)
        rest = flat - high.astype(jnp.float32)
        middle = rest.astype(jnp.bfloat16)
        low = (rest - middle.astype(jnp.float32)).astype(jnp.bfloat16)
        columns = []
        for k in range(dp):
            terms = [jnp.dot(part, held[k], preferred_element_type=jnp.float32) for part in (high, middle, low)]
            columns.append((terms[0] + terms[1] + terms[2])[0:1])
        column = jnp.concatenate(columns, axis=0)
        first = column.astype(jnp.bfloat16)
        second = (column - first.astype(jnp.float32)).astype(jnp.bfloat16)
        empty = jnp.zeros((EXTRA - 2 * column.shape[0], column.shape[1]), jnp.float32)
        extra = jnp.concatenate(
            [first.astype(jnp.float32), second.astype(jnp.float32), empty], axis=0
        ).astype(jnp.bfloat16)
        for k in range(dp):
            message_ref = messages[k].at[0] if apart else messages[0].at[k]
            message_ref[2 * rows : 3 * rows] = pre_grad
            message_ref[3 * rows : 4 * rows] = scaled
            message_ref[4 * rows :] = extra

    @pl.when(step >= steps)
    def _():
        pre_grad = messages[0][0, 2 * rows : 3 * rows]
        out = lax.dot_general(pre_grad, held_up[step - steps], trailing, preferred_element_type=jnp.float32)
        out = (out + lgs[:, 0:1] * row_ref[...]).astype(jnp.bfloat16)
        near_ref[...] = out[:half]
        far_ref[...] = out[half:]


def expert_rows(place, meta, router, router_row, near, far, w_up, w_down, dp, apart):
    rows = meta.shape[0]
    width, hid = w_up.shape
    piece = width // dp
    strip = STRIP if piece % STRIP == 0 else piece
    steps = width // strip
    held = 4 * rows + EXTRA
    shapes = [(1, held, piece)] * dp if apart else [(dp, held, piece)]
    first = lambda k: jnp.minimum(k, steps - 1)
    second = lambda k: jnp.maximum(k - steps, 0)
    weight = pl.BlockSpec((strip, hid), lambda k, place: (first(k), 0))
    block = pl.BlockSpec((near.shape[0], strip), lambda k, place: (0, first(k)))
    back = pl.BlockSpec((rows // 2, strip), lambda k, place: (0, second(k)))
    whole = lambda shape: pl.BlockSpec(shape, lambda k, place: (0,) * len(shape))
    return pl.pallas_call(
        functools.partial(expert_kernel, apart, steps),
        grid_spec=pltpu.PrefetchScalarGridSpec(
            num_scalar_prefetch=1,
            grid=(2 * steps,),
            in_specs=[
                whole(meta.shape),
                pl.BlockSpec((router.shape[0], strip), lambda k, place: (0, first(k))),
                block, block, weight, weight,
                pl.BlockSpec((1, strip), lambda k, place: (0, second(k))),
            ],
            out_specs=[whole(shape) for shape in shapes] + [back, back],
            scratch_shapes=[
                pltpu.VMEM((rows, hid), jnp.float32),
                pltpu.VMEM((rows, hid), jnp.float32),
                pltpu.VMEM((rows, router.shape[0]), jnp.float32),
                pltpu.VMEM((dp, rows, piece), jnp.bfloat16),
                pltpu.VMEM((steps, strip, hid), jnp.bfloat16),
                pltpu.VMEM((rows, 128), jnp.float32),
            ],
        ),
        out_shape=[jax.ShapeDtypeStruct(shape, jnp.bfloat16) for shape in shapes + [(rows // 2, width)] * 2],
        compiler_params=pltpu.CompilerParams(vmem_limit_bytes=VMEM_LIMIT),
        cost_estimate=SMALL,
        name="expert_rows",
    )(place, meta, router, near, far, w_up, w_down, router_row)


def weights_kernel(sizes, has_start, *refs):
    refs = list(refs)
    chunks = []
    for size in sizes:
        lefts = [refs.pop(0) for _ in range(size)]
        rights = [refs.pop(0) for _ in range(size)]
        rows = lefts[0].shape[1] // 2
        chunks.append(
            [(left.at[k], right.at[k]) for left, right in zip(lefts, rights) for k in range(left.shape[0])]
        )
    dp = len(chunks[0])
    start = [refs.pop(0) for _ in range(3)] if has_start else None
    outs = refs
    contract = (((0,), (0,)), ((), ()))
    for which in range(2):
        total = start[which][...] if has_start else None
        low = which * rows
        for pairs in chunks:
            left = jnp.concatenate([ref[low : low + rows] for ref, _ in pairs], axis=0)
            right = jnp.concatenate(
                [ref[2 * rows + low : 3 * rows + low] for _, ref in pairs], axis=0
            )
            term = lax.dot_general(left, right, contract, preferred_element_type=jnp.float32)
            total = term if total is None else total + term
        outs[which][...] = total.astype(outs[which].dtype)
    column = start[2][...] if has_start else jnp.zeros(outs[2].shape, jnp.float32)
    for pairs in chunks:
        for _, ref in pairs:
            both = ref[4 * rows :].astype(jnp.float32)
            column = column + both[:dp] + both[dp : 2 * dp]
    outs[2][...] = column


def weight_terms(chunks, rows, start, last):
    dp = sum(block.shape[0] for block in chunks[0])
    piece = chunks[0][0].shape[2]
    tile = min(piece, 256)
    kind = jnp.bfloat16 if last else jnp.float32
    strip = pl.BlockSpec((tile, piece), lambda i: (i, 0))
    column = pl.BlockSpec((dp, piece), lambda i: (0, 0))
    specs, arrays = [], []
    for blocks in chunks:
        specs += [pl.BlockSpec((block.shape[0], 2 * rows, tile), lambda i: (0, 0, i)) for block in blocks]
        specs += [pl.BlockSpec(block.shape, lambda i: (0, 0, 0)) for block in blocks]
        arrays += list(blocks) * 2
    if start is not None:
        specs += [strip, strip, column]
        arrays += list(start)
    return pl.pallas_call(
        functools.partial(weights_kernel, [len(blocks) for blocks in chunks], start is not None),
        grid=(piece // tile,),
        in_specs=specs,
        out_specs=[strip, strip, column],
        out_shape=[jax.ShapeDtypeStruct((piece, piece), kind)] * 2
        + [jax.ShapeDtypeStruct((dp, piece), jnp.float32)],
        compiler_params=pltpu.CompilerParams(vmem_limit_bytes=VMEM_LIMIT),
        cost_estimate=SMALL if last else LARGE,
        name="weight_terms",
    )(*arrays)


def combine_kernel(slots_ref, *refs):
    blocks, out_ref = refs[:-1], refs[-1]
    tok_rows = out_ref.shape[0]
    places = lax.broadcasted_iota(jnp.int32, (tok_rows, slots_ref.shape[1]), 0).astype(jnp.float32)
    picks = jnp.where(slots_ref[...] == places, 1.0, 0.0).astype(jnp.bfloat16)
    rows = jnp.concatenate([block[...] for block in blocks], axis=0)
    out_ref[...] = jnp.dot(picks, rows, preferred_element_type=jnp.float32).astype(out_ref.dtype)


def combine(slots, blocks, tok_rows):
    per_slot, width = blocks[0].shape
    tile = 1024 if width % 1024 == 0 else width
    block = pl.BlockSpec((per_slot, tile), lambda k: (0, k))
    return pl.pallas_call(
        combine_kernel,
        grid=(width // tile,),
        in_specs=[pl.BlockSpec(slots.shape, lambda k: (0, 0))] + [block] * len(blocks),
        out_specs=pl.BlockSpec((tok_rows, tile), lambda k: (0, k)),
        out_shape=jax.ShapeDtypeStruct((tok_rows, width), jnp.bfloat16),
        compiler_params=pltpu.CompilerParams(vmem_limit_bytes=VMEM_LIMIT),
        cost_estimate=SMALL,
        name="combine",
    )(slots, *blocks)


def after(block, *others):
    return lax.optimization_barrier((block,) + others)[0]


def on_line(tokens, out_grad, route_slots, expert_counts, router_weight, up_weight, down_weight):
    experts = lax.axis_size("expert")
    dp = lax.axis_size("dp")
    chips = experts // 2
    me = lax.axis_index("expert")
    chip = me // 2
    core = me % 2
    tok_rows = tokens.shape[0]
    slots = route_slots[0, 0]
    per_slot = slots.shape[1]
    w_up = up_weight[0]
    w_down = down_weight[0]
    middle = jnp.logical_and(chip >= 1, chip <= 2)

    def between(block, chip_pairs):
        pairs = [(2 * a + c, 2 * b + c) for a, b in chip_pairs for c in range(2)]
        return lax.ppermute(block, "expert", pairs)

    def across(block, mask):
        return lax.ppermute(block, "expert", [(e, e ^ mask) for e in range(experts)])

    slots_float = slots.astype(jnp.float32)
    counts = jnp.broadcast_to(expert_counts.astype(jnp.float32)[None, :], (experts, tok_rows))
    own_facts = jnp.concatenate([slots_float, counts], axis=1)
    facts = lax.all_to_all(own_facts, "expert", 0, 0, tiled=True)
    got_slots = facts[:, :per_slot]
    hits = got_slots[:, :, None] == jnp.arange(tok_rows, dtype=jnp.float32)[None, None, :]
    got_counts = jnp.sum(jnp.where(hits, facts[:, None, per_slot:], 0.0), axis=2)
    shares = jnp.where(got_slots >= 0, 1.0 / jnp.maximum(got_counts, 1.0), 0.0)
    metas = jnp.stack([got_slots, shares], axis=-1).reshape(chips, 2, per_slot, 2)
    metas = jnp.where(core == 0, metas, metas[:, ::-1]).reshape(chips, 2 * per_slot, 2)
    mine = slots_float.reshape(chips, 2, per_slot)
    mine = jnp.where(core == 0, mine, mine[:, ::-1])
    order = [chip ^ j for j in range(chips)]
    mine = jnp.concatenate([lax.dynamic_index_in_dim(mine, k, 0, False) for k in order], axis=0)

    router_row = lax.dynamic_index_in_dim(router_weight.T, me, 0, True)
    high = lax.reduce_precision(router_row, 8, 7)
    rest = router_row - high
    mid = lax.reduce_precision(rest, 8, 7)
    router = jnp.concatenate([high, mid, rest - mid, jnp.zeros((13, high.shape[1]), jnp.float32)], axis=0)
    router = router.astype(jnp.bfloat16)

    ends = [(0, 1), (1, 0), (2, 3), (3, 2)]
    inner = [(1, 2), (2, 1)]
    outward = [(1, 0), (2, 3)]

    def settle(pair):
        return pair if not isinstance(pair, tuple) else jnp.where(middle, pair[0], pair[1])

    own = after(jnp.concatenate([tokens, out_grad], axis=0), facts)
    one, inside = between(own, ends), between(own, inner)

    place = jnp.reshape(lax.axis_index("dp"), (1,)).astype(jnp.int32)

    def exchange(block):
        return lax.all_to_all(block, "dp", 0, 0, tiled=True)

    def chunk(j, pair, before, apart=False):
        near_block = settle(pair)
        far_block = across(near_block, 1)
        meta = after(lax.dynamic_index_in_dim(metas, order[j], 0, False), *before)
        *messages, near, far = expert_rows(
            place, meta, router, router_row, near_block, far_block, w_up, w_down, dp, apart
        )
        got = messages[:1] if apart else [exchange(messages[0])]
        for k in range(1, len(messages)):
            got.append(lax.ppermute(messages[k], "dp", [(q, q ^ k) for q in range(dp)]))
        return got, jnp.concatenate([near, across(far, 1)], axis=0)

    got0, back0 = chunk(0, own, ())
    inside_two, out_two = between(one, inner), between(inside, outward)
    got1, back1 = chunk(1, one, (back0,))
    out_three = between(inside_two, outward)
    got2, back2 = chunk(2, (inside_two, out_two), (back1,))
    got3, back3 = chunk(3, (inside, out_three), (back2,), apart=True)
    back1, back2 = across(back1, 2), across(back2, 4)
    back3 = across(after(back3, back1, back2), 6)
    rows = 2 * per_slot
    early = weight_terms([got0, got1, got2], rows, None, False)
    blocks = [back0, back1, back2, back3]
    up_sum, down_sum, column = weight_terms([got3], rows, early, True)
    tokens_grad = combine(mine.reshape(1, -1), blocks, tok_rows)
    return (tokens_grad, up_sum[None], down_sum[None], column.reshape(-1, 1))


def on_any(tokens, out_grad, route_slots, expert_counts, router_weight, up_weight, down_weight):
    experts = lax.axis_size("expert")
    me = lax.axis_index("expert")
    tok_rows = tokens.shape[0]
    width = tokens.shape[1]
    slots = route_slots[0, 0]
    per_slot = slots.shape[1]
    received = experts * per_slot
    contract = (((0,), (0,)), ((), ()))
    trailing = (((1,), (1,)), ((), ()))
    picks = slots[:, :, None] == jnp.arange(tok_rows, dtype=jnp.int32)[None, None, :]
    pick_half = picks.astype(jnp.bfloat16).reshape(received, tok_rows)
    gates = jax.nn.sigmoid(gate_logits(tokens, router_weight)).T
    counts = jnp.maximum(expert_counts, 1).astype(jnp.float32)[None, :]
    weight_slot = jnp.sum(jnp.where(picks, (gates / counts)[:, None, :], 0.0), axis=2)
    slope_slot = jnp.sum(jnp.where(picks, (gates * (1.0 - gates) / counts)[:, None, :], 0.0), axis=2)
    swap = lambda block: lax.all_to_all(block, "expert", split_axis=0, concat_axis=0, tiled=True)
    send_rows = jnp.dot(pick_half, tokens, preferred_element_type=jnp.float32).astype(jnp.bfloat16)
    send_grads = jnp.dot(pick_half, out_grad, preferred_element_type=jnp.float32).astype(jnp.bfloat16)
    rows_in = swap(send_rows)
    grads_in = swap(send_grads)
    facts = swap(jnp.concatenate([weight_slot, slope_slot], axis=1))
    weight_in = facts[:, :per_slot].reshape(received)
    slope_in = facts[:, per_slot:].reshape(received)
    w_up = up_weight[0]
    w_down = down_weight[0]
    pre = jnp.dot(rows_in, w_up, preferred_element_type=jnp.float32)
    active, slope = gelu_pair(pre)
    grad = jnp.dot(grads_in, w_down, preferred_element_type=jnp.float32)
    score = jnp.sum(active.astype(jnp.bfloat16).astype(jnp.float32) * grad, axis=1)
    logit_grad = score * slope_in
    pre_grad = (weight_in[:, None] * grad * slope).astype(jnp.bfloat16)
    scaled = (weight_in[:, None] * active).astype(jnp.bfloat16)
    router_row = lax.dynamic_index_in_dim(router_weight.T, me, 0, True)
    row_grad = lax.dot_general(pre_grad, w_up, trailing, preferred_element_type=jnp.float32)
    back = swap((row_grad + logit_grad[:, None] * router_row).astype(jnp.bfloat16))
    up_term = lax.dot_general(rows_in, pre_grad, contract, preferred_element_type=jnp.float32)
    down_term = lax.dot_general(grads_in, scaled, contract, preferred_element_type=jnp.float32)
    spread = lambda term: lax.psum_scatter(
        term.astype(jnp.bfloat16), "dp", scatter_dimension=0, tiled=True
    )
    tokens_grad = lax.dot_general(pick_half, back, contract, preferred_element_type=jnp.float32)
    column = jnp.sum(logit_grad[:, None] * rows_in.astype(jnp.float32), axis=0, keepdims=True)
    router_grad = lax.psum(column, "dp").T
    return (tokens_grad.astype(jnp.bfloat16), spread(up_term)[None], spread(down_term)[None], router_grad)


def solution(mesh):
    line = mesh.shape["expert"] == 8 and mesh.shape["dp"] == 4
    return jax.shard_map(
        on_line if line else on_any,
        mesh=mesh,
        in_specs=(
            P(("dp", "expert"), None),
            P(("dp", "expert"), None),
            P("dp", "expert", None, None),
            P(("dp", "expert")),
            P(),
            P("expert", None, None),
            P("expert", None, None),
        ),
        out_specs=(
            P(("dp", "expert"), None),
            P("expert", "dp", None),
            P("expert", "dp", None),
            P(None, "expert"),
        ),
        check_vma=False,
    )
```

```python
import functools

import jax
import jax.numpy as jnp
from jax import lax
from jax.experimental import pallas as pl
from jax.experimental.pallas import tpu as pltpu
from jax.sharding import PartitionSpec as P

STRIP = 1024
VMEM_LIMIT = 56 * 1024 * 1024
SMALL = pl.CostEstimate(flops=1024, bytes_accessed=1024, transcendentals=0)


def gelu_pair(values):
    inner = 0.7978845608 * (values + 0.044715 * values * values * values)
    tangent = jnp.tanh(inner)
    result = 0.5 * values * (1.0 + tangent)
    slope = 0.5 * (1.0 + tangent) + 0.5 * values * (1.0 - tangent * tangent) * 0.7978845608 * (
        1.0 + 3.0 * 0.044715 * values * values
    )
    return (result, slope)


def gate_logits(tokens, router_weight):
    high = lax.reduce_precision(router_weight, 8, 7)
    rest = router_weight - high
    middle = lax.reduce_precision(rest, 8, 7)
    low = rest - middle
    terms = jnp.concatenate([high, middle, low], axis=1).astype(jnp.bfloat16)
    parts = jnp.dot(tokens, terms, preferred_element_type=jnp.float32)
    experts = router_weight.shape[1]
    return parts[:, :experts] + parts[:, experts : 2 * experts] + parts[:, 2 * experts :]


EXTRA = 16


LARGE = pl.CostEstimate(flops=10000000000, bytes_accessed=1024, transcendentals=0)


def picks_of(meta_ref, tok_rows):
    places = lax.broadcasted_iota(jnp.int32, (meta_ref.shape[0], tok_rows), 1).astype(jnp.float32)
    return jnp.where(meta_ref[:, 0:1] == places, 1.0, 0.0).astype(jnp.bfloat16)


def pick(picks, near_ref, far_ref, first):
    half = picks.shape[0] // 2
    part = pl.ds(first, picks.shape[1])
    top = jnp.dot(picks[:half], near_ref[part], preferred_element_type=jnp.float32)
    bottom = jnp.dot(picks[half:], far_ref[part], preferred_element_type=jnp.float32)
    return jnp.concatenate([top, bottom], axis=0).astype(jnp.bfloat16)


def expert_kernel(apart, steps, place_ref, meta_ref, router_ref, *refs):
    sources, (up_ref, down_ref, row_ref), messages = refs[:2], refs[2:5], refs[5:-8]
    near_ref, far_ref, pre, back, logit, held, held_up, lgs = refs[-8:]
    step = pl.program_id(0)
    rows = meta_ref.shape[0]
    half = rows // 2
    trailing = (((1,), (1,)), ((), ()))
    tok_rows = sources[0].shape[0] // 2
    dp, _, piece = held.shape
    strip = up_ref.shape[0]
    per_piece = piece // strip

    @pl.when(step < steps)
    def _():
        picks = picks_of(meta_ref, tok_rows)
        x, g = pick(picks, *sources, 0), pick(picks, *sources, tok_rows)
        shard = step // per_piece
        lanes = pl.ds(pl.multiple_of(step % per_piece * strip, strip), strip)
        if apart:
            for k, message_ref in enumerate(messages):

                @pl.when(shard ^ place_ref[0] == k)
                def _():
                    message_ref[0, :rows, lanes] = x
                    message_ref[0, rows : 2 * rows, lanes] = g
        else:
            messages[0][shard, :rows, lanes] = x
            messages[0][shard, rows : 2 * rows, lanes] = g
        held[shard, :, lanes] = x
        held_up[step] = up_ref[...]
        pre_term = jnp.dot(x, up_ref[...], preferred_element_type=jnp.float32)
        back_term = jnp.dot(g, down_ref[...], preferred_element_type=jnp.float32)
        logit_term = lax.dot_general(x, router_ref[...], trailing, preferred_element_type=jnp.float32)

        @pl.when(step == 0)
        def _():
            pre[...] = pre_term
            back[...] = back_term
            logit[...] = logit_term

        @pl.when(step > 0)
        def _():
            pre[...] += pre_term
            back[...] += back_term
            logit[...] += logit_term

    @pl.when(step == steps - 1)
    def _():
        gate = jax.nn.sigmoid(jnp.sum(logit[...], axis=1, keepdims=True))
        weight = gate * meta_ref[:, 1:2]
        active, slope = gelu_pair(pre[...])
        grad = back[...]
        score = jnp.sum(active.astype(jnp.bfloat16).astype(jnp.float32) * grad, axis=1, keepdims=True)
        pre_grad = (weight * grad * slope).astype(jnp.bfloat16)
        scaled = (weight * active).astype(jnp.bfloat16)
        lg = score * weight * (1.0 - gate)
        lgs[...] = jnp.broadcast_to(lg, lgs.shape)
        flat = jnp.transpose(jnp.broadcast_to(lg, (rows, rows)))[:8]
        high = flat.astype(jnp.bfloat16)
        rest = flat - high.astype(jnp.float32)
        middle = rest.astype(jnp.bfloat16)
        low = (rest - middle.astype(jnp.float32)).astype(jnp.bfloat16)
        columns = []
        for k in range(dp):
            terms = [jnp.dot(part, held[k], preferred_element_type=jnp.float32) for part in (high, middle, low)]
            columns.append((terms[0] + terms[1] + terms[2])[0:1])
        column = jnp.concatenate(columns, axis=0)
        first = column.astype(jnp.bfloat16)
        second = (column - first.astype(jnp.float32)).astype(jnp.bfloat16)
        empty = jnp.zeros((EXTRA - 2 * column.shape[0], column.shape[1]), jnp.float32)
        extra = jnp.concatenate(
            [first.astype(jnp.float32), second.astype(jnp.float32), empty], axis=0
        ).astype(jnp.bfloat16)
        for k in range(dp):
            message_ref = messages[k].at[0] if apart else messages[0].at[k]
            message_ref[2 * rows : 3 * rows] = pre_grad
            message_ref[3 * rows : 4 * rows] = scaled
            message_ref[4 * rows :] = extra

    @pl.when(step >= steps)
    def _():
        pre_grad = messages[0][0, 2 * rows : 3 * rows]
        out = lax.dot_general(pre_grad, held_up[step - steps], trailing, preferred_element_type=jnp.float32)
        out = (out + lgs[:, 0:1] * row_ref[...]).astype(jnp.bfloat16)
        near_ref[...] = out[:half]
        far_ref[...] = out[half:]


def expert_rows(place, meta, router, router_row, near, far, w_up, w_down, dp, apart):
    rows = meta.shape[0]
    width, hid = w_up.shape
    piece = width // dp
    strip = STRIP if piece % STRIP == 0 else piece
    steps = width // strip
    held = 4 * rows + EXTRA
    shapes = [(1, held, piece)] * dp if apart else [(dp, held, piece)]
    first = lambda k: jnp.minimum(k, steps - 1)
    second = lambda k: jnp.maximum(k - steps, 0)
    weight = pl.BlockSpec((strip, hid), lambda k, place: (first(k), 0))
    block = pl.BlockSpec((near.shape[0], strip), lambda k, place: (0, first(k)))
    back = pl.BlockSpec((rows // 2, strip), lambda k, place: (0, second(k)))
    whole = lambda shape: pl.BlockSpec(shape, lambda k, place: (0,) * len(shape))
    return pl.pallas_call(
        functools.partial(expert_kernel, apart, steps),
        grid_spec=pltpu.PrefetchScalarGridSpec(
            num_scalar_prefetch=1,
            grid=(2 * steps,),
            in_specs=[
                whole(meta.shape),
                pl.BlockSpec((router.shape[0], strip), lambda k, place: (0, first(k))),
                block, block, weight, weight,
                pl.BlockSpec((1, strip), lambda k, place: (0, second(k))),
            ],
            out_specs=[whole(shape) for shape in shapes] + [back, back],
            scratch_shapes=[
                pltpu.VMEM((rows, hid), jnp.float32),
                pltpu.VMEM((rows, hid), jnp.float32),
                pltpu.VMEM((rows, router.shape[0]), jnp.float32),
                pltpu.VMEM((dp, rows, piece), jnp.bfloat16),
                pltpu.VMEM((steps, strip, hid), jnp.bfloat16),
                pltpu.VMEM((rows, 128), jnp.float32),
            ],
        ),
        out_shape=[jax.ShapeDtypeStruct(shape, jnp.bfloat16) for shape in shapes + [(rows // 2, width)] * 2],
        compiler_params=pltpu.CompilerParams(vmem_limit_bytes=VMEM_LIMIT),
        cost_estimate=SMALL,
        name="expert_rows",
    )(place, meta, router, near, far, w_up, w_down, router_row)


def weights_kernel(sizes, has_start, *refs):
    refs = list(refs)
    chunks = []
    for size in sizes:
        lefts = [refs.pop(0) for _ in range(size)]
        rights = [refs.pop(0) for _ in range(size)]
        rows = lefts[0].shape[1] // 2
        chunks.append(
            [(left.at[k], right.at[k]) for left, right in zip(lefts, rights) for k in range(left.shape[0])]
        )
    dp = len(chunks[0])
    start = [refs.pop(0) for _ in range(3)] if has_start else None
    outs = refs
    contract = (((0,), (0,)), ((), ()))
    for which in range(2):
        total = start[which][...] if has_start else None
        low = which * rows
        for pairs in chunks:
            left = jnp.concatenate([ref[low : low + rows] for ref, _ in pairs], axis=0)
            right = jnp.concatenate(
                [ref[2 * rows + low : 3 * rows + low] for _, ref in pairs], axis=0
            )
            term = lax.dot_general(left, right, contract, preferred_element_type=jnp.float32)
            total = term if total is None else total + term
        outs[which][...] = total.astype(outs[which].dtype)
    column = start[2][...] if has_start else jnp.zeros(outs[2].shape, jnp.float32)
    for pairs in chunks:
        for _, ref in pairs:
            both = ref[4 * rows :].astype(jnp.float32)
            column = column + both[:dp] + both[dp : 2 * dp]
    outs[2][...] = column


def weight_terms(chunks, rows, start, last):
    dp = sum(block.shape[0] for block in chunks[0])
    piece = chunks[0][0].shape[2]
    tile = min(piece, 512)
    kind = jnp.bfloat16 if last else jnp.float32
    strip = pl.BlockSpec((tile, piece), lambda i: (i, 0))
    column = pl.BlockSpec((dp, piece), lambda i: (0, 0))
    specs, arrays = [], []
    for blocks in chunks:
        specs += [pl.BlockSpec((block.shape[0], 2 * rows, tile), lambda i: (0, 0, i)) for block in blocks]
        specs += [pl.BlockSpec(block.shape, lambda i: (0, 0, 0)) for block in blocks]
        arrays += list(blocks) * 2
    if start is not None:
        specs += [strip, strip, column]
        arrays += list(start)
    return pl.pallas_call(
        functools.partial(weights_kernel, [len(blocks) for blocks in chunks], start is not None),
        grid=(piece // tile,),
        in_specs=specs,
        out_specs=[strip, strip, column],
        out_shape=[jax.ShapeDtypeStruct((piece, piece), kind)] * 2
        + [jax.ShapeDtypeStruct((dp, piece), jnp.float32)],
        compiler_params=pltpu.CompilerParams(vmem_limit_bytes=VMEM_LIMIT),
        cost_estimate=SMALL if last else LARGE,
        name="weight_terms",
    )(*arrays)


def combine_kernel(has_start, slots_ref, *refs):
    blocks, start, out_ref = refs[: len(refs) - 1 - has_start], refs[-2], refs[-1]
    tok_rows = out_ref.shape[0]
    places = lax.broadcasted_iota(jnp.int32, (tok_rows, slots_ref.shape[1]), 0).astype(jnp.float32)
    picks = jnp.where(slots_ref[...] == places, 1.0, 0.0).astype(jnp.bfloat16)
    rows = jnp.concatenate([block[...] for block in blocks], axis=0)
    total = jnp.dot(picks, rows, preferred_element_type=jnp.float32)
    if has_start:
        total = total + start[...]
    out_ref[...] = total.astype(out_ref.dtype)


def combine(slots, blocks, tok_rows, start, kind):
    count, width = blocks[0].shape
    tile = 2048 if width % 2048 == 0 else width
    block = pl.BlockSpec((count, tile), lambda k: (0, k))
    strip = pl.BlockSpec((tok_rows, tile), lambda k: (0, k))
    starts = [] if start is None else [start]
    return pl.pallas_call(
        functools.partial(combine_kernel, len(starts)),
        grid=(width // tile,),
        in_specs=[pl.BlockSpec(slots.shape, lambda k: (0, 0))] + [block] * len(blocks) + [strip] * len(starts),
        out_specs=strip,
        out_shape=jax.ShapeDtypeStruct((tok_rows, width), kind),
        compiler_params=pltpu.CompilerParams(vmem_limit_bytes=VMEM_LIMIT),
        cost_estimate=SMALL,
        name="combine",
    )(slots, *blocks, *starts)


def after(block, *others):
    return lax.optimization_barrier((block,) + others)[0]


def on_line(tokens, out_grad, route_slots, expert_counts, router_weight, up_weight, down_weight):
    experts = lax.axis_size("expert")
    dp = lax.axis_size("dp")
    chips = experts // 2
    me = lax.axis_index("expert")
    chip = me // 2
    core = me % 2
    tok_rows = tokens.shape[0]
    slots = route_slots[0, 0]
    per_slot = slots.shape[1]
    w_up = up_weight[0]
    w_down = down_weight[0]
    middle = jnp.logical_and(chip >= 1, chip <= 2)

    def between(block, chip_pairs):
        pairs = [(2 * a + c, 2 * b + c) for a, b in chip_pairs for c in range(2)]
        return lax.ppermute(block, "expert", pairs)

    def across(block, mask):
        return lax.ppermute(block, "expert", [(e, e ^ mask) for e in range(experts)])

    slots_float = slots.astype(jnp.float32)
    counts = jnp.broadcast_to(expert_counts.astype(jnp.float32)[None, :], (experts, tok_rows))
    own_facts = jnp.concatenate([slots_float, counts], axis=1)
    facts = lax.all_to_all(own_facts, "expert", 0, 0, tiled=True)
    got_slots = facts[:, :per_slot]
    hits = got_slots[:, :, None] == jnp.arange(tok_rows, dtype=jnp.float32)[None, None, :]
    got_counts = jnp.sum(jnp.where(hits, facts[:, None, per_slot:], 0.0), axis=2)
    shares = jnp.where(got_slots >= 0, 1.0 / jnp.maximum(got_counts, 1.0), 0.0)
    metas = jnp.stack([got_slots, shares], axis=-1).reshape(chips, 2, per_slot, 2)
    metas = jnp.where(core == 0, metas, metas[:, ::-1]).reshape(chips, 2 * per_slot, 2)
    mine = slots_float.reshape(chips, 2, per_slot)
    mine = jnp.where(core == 0, mine, mine[:, ::-1])
    order = [chip ^ j for j in range(chips)]
    mine = jnp.concatenate([lax.dynamic_index_in_dim(mine, k, 0, False) for k in order], axis=0)

    router_row = lax.dynamic_index_in_dim(router_weight.T, me, 0, True)
    high = lax.reduce_precision(router_row, 8, 7)
    rest = router_row - high
    mid = lax.reduce_precision(rest, 8, 7)
    router = jnp.concatenate([high, mid, rest - mid, jnp.zeros((13, high.shape[1]), jnp.float32)], axis=0)
    router = router.astype(jnp.bfloat16)

    ends = [(0, 1), (1, 0), (2, 3), (3, 2)]
    inner = [(1, 2), (2, 1)]
    outward = [(1, 0), (2, 3)]

    def settle(pair):
        return pair if not isinstance(pair, tuple) else jnp.where(middle, pair[0], pair[1])

    own = after(jnp.concatenate([tokens, out_grad], axis=0), facts)
    one, inside = between(own, ends), between(own, inner)

    place = jnp.reshape(lax.axis_index("dp"), (1,)).astype(jnp.int32)

    def exchange(block):
        return lax.all_to_all(block, "dp", 0, 0, tiled=True)

    def chunk(j, pair, before, apart=False):
        near_block = settle(pair)
        far_block = across(near_block, 1)
        meta = after(lax.dynamic_index_in_dim(metas, order[j], 0, False), *before)
        *messages, near, far = expert_rows(
            place, meta, router, router_row, near_block, far_block, w_up, w_down, dp, apart
        )
        got = messages[:1] if apart else [exchange(messages[0])]
        for k in range(1, len(messages)):
            got.append(lax.ppermute(messages[k], "dp", [(q, q ^ k) for q in range(dp)]))
        return got, jnp.concatenate([near, across(far, 1)], axis=0)

    got0, back0 = chunk(0, own, ())
    inside_two, out_two = between(one, inner), between(inside, outward)
    got1, back1 = chunk(1, one, (back0,))
    out_three = between(inside_two, outward)
    got2, back2 = chunk(2, (inside_two, out_two), (back1,))
    got3, back3 = chunk(3, (inside, out_three), (back2,), apart=True)
    back1, back2 = across(back1, 2), across(back2, 4)
    back3 = across(after(back3, back1, back2), 6)
    rows = 2 * per_slot
    early = weight_terms([got0, got1, got2], rows, None, False)
    lists = mine.reshape(1, -1)
    most = 3 * rows
    partial = combine(lists[:, :most], [back0, back1, back2], tok_rows, None, jnp.float32)
    partial, first = lax.optimization_barrier((partial, early[0]))
    up_sum, down_sum, column = weight_terms([got3], rows, (first, early[1], early[2]), True)
    tokens_grad = combine(lists[:, most:], [back3], tok_rows, partial, jnp.bfloat16)
    return (tokens_grad, up_sum[None], down_sum[None], column.reshape(-1, 1))


def on_any(tokens, out_grad, route_slots, expert_counts, router_weight, up_weight, down_weight):
    experts = lax.axis_size("expert")
    me = lax.axis_index("expert")
    tok_rows = tokens.shape[0]
    width = tokens.shape[1]
    slots = route_slots[0, 0]
    per_slot = slots.shape[1]
    received = experts * per_slot
    contract = (((0,), (0,)), ((), ()))
    trailing = (((1,), (1,)), ((), ()))
    picks = slots[:, :, None] == jnp.arange(tok_rows, dtype=jnp.int32)[None, None, :]
    pick_half = picks.astype(jnp.bfloat16).reshape(received, tok_rows)
    gates = jax.nn.sigmoid(gate_logits(tokens, router_weight)).T
    counts = jnp.maximum(expert_counts, 1).astype(jnp.float32)[None, :]
    weight_slot = jnp.sum(jnp.where(picks, (gates / counts)[:, None, :], 0.0), axis=2)
    slope_slot = jnp.sum(jnp.where(picks, (gates * (1.0 - gates) / counts)[:, None, :], 0.0), axis=2)
    swap = lambda block: lax.all_to_all(block, "expert", split_axis=0, concat_axis=0, tiled=True)
    send_rows = jnp.dot(pick_half, tokens, preferred_element_type=jnp.float32).astype(jnp.bfloat16)
    send_grads = jnp.dot(pick_half, out_grad, preferred_element_type=jnp.float32).astype(jnp.bfloat16)
    rows_in = swap(send_rows)
    grads_in = swap(send_grads)
    facts = swap(jnp.concatenate([weight_slot, slope_slot], axis=1))
    weight_in = facts[:, :per_slot].reshape(received)
    slope_in = facts[:, per_slot:].reshape(received)
    w_up = up_weight[0]
    w_down = down_weight[0]
    pre = jnp.dot(rows_in, w_up, preferred_element_type=jnp.float32)
    active, slope = gelu_pair(pre)
    grad = jnp.dot(grads_in, w_down, preferred_element_type=jnp.float32)
    score = jnp.sum(active.astype(jnp.bfloat16).astype(jnp.float32) * grad, axis=1)
    logit_grad = score * slope_in
    pre_grad = (weight_in[:, None] * grad * slope).astype(jnp.bfloat16)
    scaled = (weight_in[:, None] * active).astype(jnp.bfloat16)
    router_row = lax.dynamic_index_in_dim(router_weight.T, me, 0, True)
    row_grad = lax.dot_general(pre_grad, w_up, trailing, preferred_element_type=jnp.float32)
    back = swap((row_grad + logit_grad[:, None] * router_row).astype(jnp.bfloat16))
    up_term = lax.dot_general(rows_in, pre_grad, contract, preferred_element_type=jnp.float32)
    down_term = lax.dot_general(grads_in, scaled, contract, preferred_element_type=jnp.float32)
    spread = lambda term: lax.psum_scatter(
        term.astype(jnp.bfloat16), "dp", scatter_dimension=0, tiled=True
    )
    tokens_grad = lax.dot_general(pick_half, back, contract, preferred_element_type=jnp.float32)
    column = jnp.sum(logit_grad[:, None] * rows_in.astype(jnp.float32), axis=0, keepdims=True)
    router_grad = lax.psum(column, "dp").T
    return (tokens_grad.astype(jnp.bfloat16), spread(up_term)[None], spread(down_term)[None], router_grad)


def solution(mesh):
    line = mesh.shape["expert"] == 8 and mesh.shape["dp"] == 4
    return jax.shard_map(
        on_line if line else on_any,
        mesh=mesh,
        in_specs=(
            P(("dp", "expert"), None),
            P(("dp", "expert"), None),
            P("dp", "expert", None, None),
            P(("dp", "expert")),
            P(),
            P("expert", None, None),
            P("expert", None, None),
        ),
        out_specs=(
            P(("dp", "expert"), None),
            P("expert", "dp", None),
            P("expert", "dp", None),
            P(None, "expert"),
        ),
        check_vma=False,
    )
```

```python
import functools

import jax
import jax.numpy as jnp
from jax import lax
from jax.experimental import pallas as pl
from jax.experimental.pallas import tpu as pltpu
from jax.sharding import PartitionSpec as P

STRIP = 1024
VMEM_LIMIT = 56 * 1024 * 1024
SMALL = pl.CostEstimate(flops=1024, bytes_accessed=1024, transcendentals=0)


def gelu_pair(values):
    inner = 0.7978845608 * (values + 0.044715 * values * values * values)
    tangent = jnp.tanh(inner)
    result = 0.5 * values * (1.0 + tangent)
    slope = 0.5 * (1.0 + tangent) + 0.5 * values * (1.0 - tangent * tangent) * 0.7978845608 * (
        1.0 + 3.0 * 0.044715 * values * values
    )
    return (result, slope)


def gate_logits(tokens, router_weight):
    high = lax.reduce_precision(router_weight, 8, 7)
    rest = router_weight - high
    middle = lax.reduce_precision(rest, 8, 7)
    low = rest - middle
    terms = jnp.concatenate([high, middle, low], axis=1).astype(jnp.bfloat16)
    parts = jnp.dot(tokens, terms, preferred_element_type=jnp.float32)
    experts = router_weight.shape[1]
    return parts[:, :experts] + parts[:, experts : 2 * experts] + parts[:, 2 * experts :]


EXTRA = 16


LARGE = pl.CostEstimate(flops=10000000000, bytes_accessed=1024, transcendentals=0)


def picks_of(meta_ref, tok_rows):
    places = lax.broadcasted_iota(jnp.int32, (meta_ref.shape[0], tok_rows), 1).astype(jnp.float32)
    return jnp.where(meta_ref[:, 0:1] == places, 1.0, 0.0).astype(jnp.bfloat16)


def pick(picks, near_ref, far_ref, first):
    half = picks.shape[0] // 2
    part = pl.ds(first, picks.shape[1])
    top = jnp.dot(picks[:half], near_ref[part], preferred_element_type=jnp.float32)
    bottom = jnp.dot(picks[half:], far_ref[part], preferred_element_type=jnp.float32)
    return jnp.concatenate([top, bottom], axis=0).astype(jnp.bfloat16)


def expert_kernel(apart, steps, place_ref, meta_ref, router_ref, *refs):
    sources, (up_ref, down_ref, row_ref), messages = refs[:2], refs[2:5], refs[5:-8]
    near_ref, far_ref, pre, back, logit, held, held_up, lgs = refs[-8:]
    step = pl.program_id(0)
    rows = meta_ref.shape[0]
    half = rows // 2
    trailing = (((1,), (1,)), ((), ()))
    tok_rows = sources[0].shape[0] // 2
    dp, _, piece = held.shape
    strip = up_ref.shape[0]
    per_piece = piece // strip

    @pl.when(step < steps)
    def _():
        picks = picks_of(meta_ref, tok_rows)
        x, g = pick(picks, *sources, 0), pick(picks, *sources, tok_rows)
        shard = step // per_piece
        lanes = pl.ds(pl.multiple_of(step % per_piece * strip, strip), strip)
        if apart:
            for k, message_ref in enumerate(messages):

                @pl.when(shard ^ place_ref[0] == k)
                def _():
                    message_ref[0, :rows, lanes] = x
                    message_ref[0, rows : 2 * rows, lanes] = g
        else:
            messages[0][shard, :rows, lanes] = x
            messages[0][shard, rows : 2 * rows, lanes] = g
        held[shard, :, lanes] = x
        held_up[step] = up_ref[...]
        pre_term = jnp.dot(x, up_ref[...], preferred_element_type=jnp.float32)
        back_term = jnp.dot(g, down_ref[...], preferred_element_type=jnp.float32)
        logit_term = lax.dot_general(x, router_ref[...], trailing, preferred_element_type=jnp.float32)

        @pl.when(step == 0)
        def _():
            pre[...] = pre_term
            back[...] = back_term
            logit[...] = logit_term

        @pl.when(step > 0)
        def _():
            pre[...] += pre_term
            back[...] += back_term
            logit[...] += logit_term

    @pl.when(step == steps - 1)
    def _():
        gate = jax.nn.sigmoid(jnp.sum(logit[...], axis=1, keepdims=True))
        weight = gate * meta_ref[:, 1:2]
        active, slope = gelu_pair(pre[...])
        grad = back[...]
        score = jnp.sum(active.astype(jnp.bfloat16).astype(jnp.float32) * grad, axis=1, keepdims=True)
        pre_grad = (weight * grad * slope).astype(jnp.bfloat16)
        scaled = (weight * active).astype(jnp.bfloat16)
        lg = score * weight * (1.0 - gate)
        lgs[...] = jnp.broadcast_to(lg, lgs.shape)
        flat = jnp.transpose(jnp.broadcast_to(lg, (rows, rows)))[:8]
        high = flat.astype(jnp.bfloat16)
        rest = flat - high.astype(jnp.float32)
        middle = rest.astype(jnp.bfloat16)
        low = (rest - middle.astype(jnp.float32)).astype(jnp.bfloat16)
        columns = []
        for k in range(dp):
            terms = [jnp.dot(part, held[k], preferred_element_type=jnp.float32) for part in (high, middle, low)]
            columns.append((terms[0] + terms[1] + terms[2])[0:1])
        column = jnp.concatenate(columns, axis=0)
        first = column.astype(jnp.bfloat16)
        second = (column - first.astype(jnp.float32)).astype(jnp.bfloat16)
        empty = jnp.zeros((EXTRA - 2 * column.shape[0], column.shape[1]), jnp.float32)
        extra = jnp.concatenate(
            [first.astype(jnp.float32), second.astype(jnp.float32), empty], axis=0
        ).astype(jnp.bfloat16)
        for k in range(dp):
            message_ref = messages[k].at[0] if apart else messages[0].at[k]
            message_ref[2 * rows : 3 * rows] = pre_grad
            message_ref[3 * rows : 4 * rows] = scaled
            message_ref[4 * rows :] = extra

    @pl.when(step >= steps)
    def _():
        pre_grad = messages[0][0, 2 * rows : 3 * rows]
        out = lax.dot_general(pre_grad, held_up[step - steps], trailing, preferred_element_type=jnp.float32)
        out = (out + lgs[:, 0:1] * row_ref[...]).astype(jnp.bfloat16)
        near_ref[...] = out[:half]
        far_ref[...] = out[half:]


def expert_rows(place, meta, router, router_row, near, far, w_up, w_down, dp, apart):
    rows = meta.shape[0]
    width, hid = w_up.shape
    piece = width // dp
    strip = STRIP if piece % STRIP == 0 else piece
    steps = width // strip
    held = 4 * rows + EXTRA
    shapes = [(1, held, piece)] * dp if apart else [(dp, held, piece)]
    first = lambda k: jnp.minimum(k, steps - 1)
    second = lambda k: jnp.maximum(k - steps, 0)
    weight = pl.BlockSpec((strip, hid), lambda k, place: (first(k), 0))
    block = pl.BlockSpec((near.shape[0], strip), lambda k, place: (0, first(k)))
    back = pl.BlockSpec((rows // 2, strip), lambda k, place: (0, second(k)))
    whole = lambda shape: pl.BlockSpec(shape, lambda k, place: (0,) * len(shape))
    return pl.pallas_call(
        functools.partial(expert_kernel, apart, steps),
        grid_spec=pltpu.PrefetchScalarGridSpec(
            num_scalar_prefetch=1,
            grid=(2 * steps,),
            in_specs=[
                whole(meta.shape),
                pl.BlockSpec((router.shape[0], strip), lambda k, place: (0, first(k))),
                block, block, weight, weight,
                pl.BlockSpec((1, strip), lambda k, place: (0, second(k))),
            ],
            out_specs=[whole(shape) for shape in shapes] + [back, back],
            scratch_shapes=[
                pltpu.VMEM((rows, hid), jnp.float32),
                pltpu.VMEM((rows, hid), jnp.float32),
                pltpu.VMEM((rows, router.shape[0]), jnp.float32),
                pltpu.VMEM((dp, rows, piece), jnp.bfloat16),
                pltpu.VMEM((steps, strip, hid), jnp.bfloat16),
                pltpu.VMEM((rows, 128), jnp.float32),
            ],
        ),
        out_shape=[jax.ShapeDtypeStruct(shape, jnp.bfloat16) for shape in shapes + [(rows // 2, width)] * 2],
        compiler_params=pltpu.CompilerParams(vmem_limit_bytes=VMEM_LIMIT),
        cost_estimate=SMALL,
        name="expert_rows",
    )(place, meta, router, near, far, w_up, w_down, router_row)


def weights_kernel(sizes, has_start, *refs):
    refs = list(refs)
    chunks = []
    for size in sizes:
        lefts = [refs.pop(0) for _ in range(size)]
        rights = [refs.pop(0) for _ in range(size)]
        rows = lefts[0].shape[1] // 2
        chunks.append(
            [(left.at[k], right.at[k]) for left, right in zip(lefts, rights) for k in range(left.shape[0])]
        )
    start = [refs.pop(0) for _ in range(3)] if has_start else None
    outs = refs
    pieces = outs[2].shape[0]
    contract = (((0,), (0,)), ((), ()))
    for which in range(2):
        total = start[which][...] if has_start else None
        low = which * rows
        for pairs in chunks:
            left = jnp.concatenate([ref[low : low + rows] for ref, _ in pairs], axis=0)
            right = jnp.concatenate(
                [ref[2 * rows + low : 3 * rows + low] for _, ref in pairs], axis=0
            )
            term = lax.dot_general(left, right, contract, preferred_element_type=jnp.float32)
            total = term if total is None else total + term
        outs[which][...] = total.astype(outs[which].dtype)
    column = start[2][...] if has_start else jnp.zeros(outs[2].shape, jnp.float32)
    for pairs in chunks:
        for _, ref in pairs:
            both = ref[4 * rows :].astype(jnp.float32)
            column = column + both[:pieces] + both[pieces : 2 * pieces]
    outs[2][...] = column


def weight_terms(chunks, rows, start, last):
    piece = chunks[0][0].shape[2]
    tile = min(piece, 512)
    kind = jnp.bfloat16 if last else jnp.float32
    strip = pl.BlockSpec((tile, piece), lambda i: (i, 0))
    pieces = sum(block.shape[0] for block in chunks[0]) if start is None else start[2].shape[0]
    column = pl.BlockSpec((pieces, piece), lambda i: (0, 0))
    specs, arrays = [], []
    for blocks in chunks:
        specs += [pl.BlockSpec((block.shape[0], 2 * rows, tile), lambda i: (0, 0, i)) for block in blocks]
        specs += [pl.BlockSpec(block.shape, lambda i: (0, 0, 0)) for block in blocks]
        arrays += list(blocks) * 2
    if start is not None:
        specs += [strip, strip, column]
        arrays += list(start)
    return pl.pallas_call(
        functools.partial(weights_kernel, [len(blocks) for blocks in chunks], start is not None),
        grid=(piece // tile,),
        in_specs=specs,
        out_specs=[strip, strip, column],
        out_shape=[jax.ShapeDtypeStruct((piece, piece), kind)] * 2
        + [jax.ShapeDtypeStruct((pieces, piece), jnp.float32)],
        compiler_params=pltpu.CompilerParams(vmem_limit_bytes=VMEM_LIMIT),
        cost_estimate=SMALL if last else LARGE,
        name="weight_terms",
    )(*arrays)


def combine_kernel(has_start, slots_ref, *refs):
    blocks, start, out_ref = refs[: len(refs) - 1 - has_start], refs[-2], refs[-1]
    tok_rows = out_ref.shape[0]
    places = lax.broadcasted_iota(jnp.int32, (tok_rows, slots_ref.shape[1]), 0).astype(jnp.float32)
    picks = jnp.where(slots_ref[...] == places, 1.0, 0.0).astype(jnp.bfloat16)
    rows = jnp.concatenate([block[...] for block in blocks], axis=0)
    total = jnp.dot(picks, rows, preferred_element_type=jnp.float32)
    if has_start:
        total = total + start[...]
    out_ref[...] = total.astype(out_ref.dtype)


def combine(slots, blocks, tok_rows, start, kind):
    count, width = blocks[0].shape
    tile = 2048 if width % 2048 == 0 else width
    block = pl.BlockSpec((count, tile), lambda k: (0, k))
    strip = pl.BlockSpec((tok_rows, tile), lambda k: (0, k))
    starts = [] if start is None else [start]
    return pl.pallas_call(
        functools.partial(combine_kernel, len(starts)),
        grid=(width // tile,),
        in_specs=[pl.BlockSpec(slots.shape, lambda k: (0, 0))] + [block] * len(blocks) + [strip] * len(starts),
        out_specs=strip,
        out_shape=jax.ShapeDtypeStruct((tok_rows, width), kind),
        compiler_params=pltpu.CompilerParams(vmem_limit_bytes=VMEM_LIMIT),
        cost_estimate=SMALL,
        name="combine",
    )(slots, *blocks, *starts)


def after(block, *others):
    return lax.optimization_barrier((block,) + others)[0]


def on_line(tokens, out_grad, route_slots, expert_counts, router_weight, up_weight, down_weight):
    experts = lax.axis_size("expert")
    dp = lax.axis_size("dp")
    chips = experts // 2
    me = lax.axis_index("expert")
    chip = me // 2
    core = me % 2
    tok_rows = tokens.shape[0]
    slots = route_slots[0, 0]
    per_slot = slots.shape[1]
    w_up = up_weight[0]
    w_down = down_weight[0]
    middle = jnp.logical_and(chip >= 1, chip <= 2)

    def between(block, chip_pairs):
        pairs = [(2 * a + c, 2 * b + c) for a, b in chip_pairs for c in range(2)]
        return lax.ppermute(block, "expert", pairs)

    def across(block, mask):
        return lax.ppermute(block, "expert", [(e, e ^ mask) for e in range(experts)])

    slots_float = slots.astype(jnp.float32)
    counts = jnp.broadcast_to(expert_counts.astype(jnp.float32)[None, :], (experts, tok_rows))
    own_facts = jnp.concatenate([slots_float, counts], axis=1)
    facts = lax.all_to_all(own_facts, "expert", 0, 0, tiled=True)
    got_slots = facts[:, :per_slot]
    hits = got_slots[:, :, None] == jnp.arange(tok_rows, dtype=jnp.float32)[None, None, :]
    got_counts = jnp.sum(jnp.where(hits, facts[:, None, per_slot:], 0.0), axis=2)
    shares = jnp.where(got_slots >= 0, 1.0 / jnp.maximum(got_counts, 1.0), 0.0)
    metas = jnp.stack([got_slots, shares], axis=-1).reshape(chips, 2, per_slot, 2)
    metas = jnp.where(core == 0, metas, metas[:, ::-1]).reshape(chips, 2 * per_slot, 2)
    mine = slots_float.reshape(chips, 2, per_slot)
    mine = jnp.where(core == 0, mine, mine[:, ::-1])
    order = [chip ^ j for j in range(chips)]
    mine = jnp.concatenate([lax.dynamic_index_in_dim(mine, k, 0, False) for k in order], axis=0)

    router_row = lax.dynamic_index_in_dim(router_weight.T, me, 0, True)
    high = lax.reduce_precision(router_row, 8, 7)
    rest = router_row - high
    mid = lax.reduce_precision(rest, 8, 7)
    router = jnp.concatenate([high, mid, rest - mid, jnp.zeros((13, high.shape[1]), jnp.float32)], axis=0)
    router = router.astype(jnp.bfloat16)

    ends = [(0, 1), (1, 0), (2, 3), (3, 2)]
    inner = [(1, 2), (2, 1)]
    outward = [(1, 0), (2, 3)]

    def settle(pair):
        return pair if not isinstance(pair, tuple) else jnp.where(middle, pair[0], pair[1])

    own = after(jnp.concatenate([tokens, out_grad], axis=0), facts)
    one, inside = between(own, ends), between(own, inner)

    place = jnp.reshape(lax.axis_index("dp"), (1,)).astype(jnp.int32)

    def exchange(block):
        return lax.all_to_all(block, "dp", 0, 0, tiled=True)

    def chunk(j, pair, before, apart=False):
        near_block = settle(pair)
        far_block = across(near_block, 1)
        meta = after(lax.dynamic_index_in_dim(metas, order[j], 0, False), *before)
        *messages, near, far = expert_rows(
            place, meta, router, router_row, near_block, far_block, w_up, w_down, dp, apart
        )
        got = messages[:1] if apart else [exchange(messages[0])]
        for k in range(1, len(messages)):
            got.append(lax.ppermute(messages[k], "dp", [(q, q ^ k) for q in range(dp)]))
        return got, jnp.concatenate([near, across(far, 1)], axis=0)

    got0, back0 = chunk(0, own, ())
    inside_two, out_two = between(one, inner), between(inside, outward)
    got1, back1 = chunk(1, one, (back0,))
    out_three = between(inside_two, outward)
    got2, back2 = chunk(2, (inside_two, out_two), (back1,))
    got3, back3 = chunk(3, (inside, out_three), (back2,), apart=True)
    back1, back2 = across(back1, 2), across(back2, 4)
    back3 = across(after(back3, back1, back2), 6)
    rows = 2 * per_slot
    early = weight_terms([got0, got1, got2, got3[:1]], rows, None, False)
    lists = mine.reshape(1, -1)
    most = 3 * rows
    partial = combine(lists[:, :most], [back0, back1, back2], tok_rows, None, jnp.float32)
    partial, first = lax.optimization_barrier((partial, early[0]))
    up_sum, down_sum, column = weight_terms([got3[1:]], rows, (first, early[1], early[2]), True)
    tokens_grad = combine(lists[:, most:], [back3], tok_rows, partial, jnp.bfloat16)
    return (tokens_grad, up_sum[None], down_sum[None], column.reshape(-1, 1))


def on_any(tokens, out_grad, route_slots, expert_counts, router_weight, up_weight, down_weight):
    experts = lax.axis_size("expert")
    me = lax.axis_index("expert")
    tok_rows = tokens.shape[0]
    width = tokens.shape[1]
    slots = route_slots[0, 0]
    per_slot = slots.shape[1]
    received = experts * per_slot
    contract = (((0,), (0,)), ((), ()))
    trailing = (((1,), (1,)), ((), ()))
    picks = slots[:, :, None] == jnp.arange(tok_rows, dtype=jnp.int32)[None, None, :]
    pick_half = picks.astype(jnp.bfloat16).reshape(received, tok_rows)
    gates = jax.nn.sigmoid(gate_logits(tokens, router_weight)).T
    counts = jnp.maximum(expert_counts, 1).astype(jnp.float32)[None, :]
    weight_slot = jnp.sum(jnp.where(picks, (gates / counts)[:, None, :], 0.0), axis=2)
    slope_slot = jnp.sum(jnp.where(picks, (gates * (1.0 - gates) / counts)[:, None, :], 0.0), axis=2)
    swap = lambda block: lax.all_to_all(block, "expert", split_axis=0, concat_axis=0, tiled=True)
    send_rows = jnp.dot(pick_half, tokens, preferred_element_type=jnp.float32).astype(jnp.bfloat16)
    send_grads = jnp.dot(pick_half, out_grad, preferred_element_type=jnp.float32).astype(jnp.bfloat16)
    rows_in = swap(send_rows)
    grads_in = swap(send_grads)
    facts = swap(jnp.concatenate([weight_slot, slope_slot], axis=1))
    weight_in = facts[:, :per_slot].reshape(received)
    slope_in = facts[:, per_slot:].reshape(received)
    w_up = up_weight[0]
    w_down = down_weight[0]
    pre = jnp.dot(rows_in, w_up, preferred_element_type=jnp.float32)
    active, slope = gelu_pair(pre)
    grad = jnp.dot(grads_in, w_down, preferred_element_type=jnp.float32)
    score = jnp.sum(active.astype(jnp.bfloat16).astype(jnp.float32) * grad, axis=1)
    logit_grad = score * slope_in
    pre_grad = (weight_in[:, None] * grad * slope).astype(jnp.bfloat16)
    scaled = (weight_in[:, None] * active).astype(jnp.bfloat16)
    router_row = lax.dynamic_index_in_dim(router_weight.T, me, 0, True)
    row_grad = lax.dot_general(pre_grad, w_up, trailing, preferred_element_type=jnp.float32)
    back = swap((row_grad + logit_grad[:, None] * router_row).astype(jnp.bfloat16))
    up_term = lax.dot_general(rows_in, pre_grad, contract, preferred_element_type=jnp.float32)
    down_term = lax.dot_general(grads_in, scaled, contract, preferred_element_type=jnp.float32)
    spread = lambda term: lax.psum_scatter(
        term.astype(jnp.bfloat16), "dp", scatter_dimension=0, tiled=True
    )
    tokens_grad = lax.dot_general(pick_half, back, contract, preferred_element_type=jnp.float32)
    column = jnp.sum(logit_grad[:, None] * rows_in.astype(jnp.float32), axis=0, keepdims=True)
    router_grad = lax.psum(column, "dp").T
    return (tokens_grad.astype(jnp.bfloat16), spread(up_term)[None], spread(down_term)[None], router_grad)


def solution(mesh):
    line = mesh.shape["expert"] == 8 and mesh.shape["dp"] == 4
    return jax.shard_map(
        on_line if line else on_any,
        mesh=mesh,
        in_specs=(
            P(("dp", "expert"), None),
            P(("dp", "expert"), None),
            P("dp", "expert", None, None),
            P(("dp", "expert")),
            P(),
            P("expert", None, None),
            P("expert", None, None),
        ),
        out_specs=(
            P(("dp", "expert"), None),
            P("expert", "dp", None),
            P("expert", "dp", None),
            P(None, "expert"),
        ),
        check_vma=False,
    )
```
